768 devices in a mesh: seq: 16 (over y_lo, x, core), grp: 48 (over z, y_hi).
Axes of the slice: x: 4, y: 8 (y_hi: 4, y_lo: 2; y = y_hi * 2 + y_lo), z: 12, core: 2. Of those that a mesh axis runs over, the one named last changes fastest.
Arguments:
- tokens: bfloat16 [48, 2048, 1408], P('grp', 'seq'), may hold values from -6 to 6
- target_kv: bfloat16 [1408, 1408], P('seq'), may hold values from -0.15625 to 0.15625
- context_kv: bfloat16 [1408, 1408], P('seq'), may hold values from -0.15625 to 0.15625
- query_weight: bfloat16 [704, 1408], replicated, may hold values from -0.15625 to 0.15625
- pred_hidden: bfloat16 [48, 2048, 384], P('grp', 'seq'), may hold values from -6 to 6
- pred_weight: bfloat16 [48, 704, 384], P('grp'), may hold values from -0.3125 to 0.3125
- target_mask: int32 [48, 1024], P('grp', 'seq'), may hold values 0 or 1
- owners: int32 [48, 1024, 1], P('grp', 'seq'), may hold values from 0 to 47; in each aligned block of 64 rows (0 to 63, 64 to 127, ..., all dimensions but the last counted through in order) at most 2 rows name the same one
Outputs:
- new_kv: bfloat16 [1408, 1408], P('seq')
- targets: bfloat16 [48, 2048, 704], P('grp', 'seq')
- pred_grad: bfloat16 [48, 2048, 384], P('grp', 'seq')
The draws below stay inside these ranges and needn't reach their ends.
Inputs may be any that keep to these rules, and one draw needn't show every extreme that they name: `owners`: among the 64 token pairs of one device no owner is named more than 2 times, a bound that some block reaches.
All inputs are finite; a program needn't handle non-finite values. No bound on the sum of `target_mask` on one device may be relied on, other than what follows from the above.
Results may differ from the reference program's by a relative error of at most 0.011.
Values may be sent and summed in bfloat16 or wider, within the bound.
A program may use at most 64 MiB of HBM per device.

```python
import math
import jax
import jax.numpy as jnp
import numpy as np
from jax import lax

D = 1408
HEAD = 64
HEADS = 11
PRED = 384
ATT = 704
CLIP_TOK = 2048
CLIPS = 48
BLOCKS_DEV = 64
BLOCKS = 1024
CAP = 2
EXPERTS = 48


def plant(entries, own_key, low, top_value):
    longest = entries.shape.index(max(entries.shape))
    spots = []
    for shift in (0, 1):
        where = [jax.random.randint(jax.random.fold_in(own_key, axis), (), 0, length) for axis, length in enumerate(entries.shape)]
        where[longest] = (where[longest] + shift) % entries.shape[longest]
        spots.append(tuple(where))
    return entries.at[spots[0]].set(low).at[spots[1]].set(top_value)


def shard_levels(stream_key, extent, split, least, largest):
    level = 1.0
    for dim, shards_of in split:
        draws = jax.random.uniform(jax.random.fold_in(jax.random.fold_in(stream_key, 6), dim), (shards_of,), jnp.float32, least / len(split), largest / len(split))
        level = level * jnp.repeat(jnp.exp(draws), extent[dim] // shards_of).reshape((-1,) + (1,) * (len(extent) - 1 - dim))
    return level


def shared_out(stream_key, own, number, rows, amount, top, reach, skew):
    ranking = jax.random.permutation(stream_key, amount)
    packed, usual = load_shares(amount, rows * top, reach, skew, True), load_shares(amount, rows * top, reach, skew, False)
    places = jnp.arange(amount)

    def named(tallies, offset_by):
        used = int((tallies > 0).sum())
        fixed = max(1, used // 4)
        passed = fixed + (places - fixed + offset_by * (used - fixed)) % max(1, amount - fixed)
        return jnp.zeros((amount,), jnp.int32).at[ranking[jnp.where(places < fixed, places, passed)]].set(jnp.asarray(tallies, jnp.int32))

    tallies = jnp.where(number % 4 == 0, named(packed, number // 4), named(usual, number - number // 4 - 1))
    mixed = jax.random.permutation(jax.random.fold_in(own, 3), amount)
    donor, receiver = mixed[0:amount // 2 * 2:2], mixed[1:amount // 2 * 2:2]
    room = jnp.minimum(tallies[donor] - 1, reach - tallies[receiver]) // 2
    room = jnp.where((donor == ranking[0]) | (receiver == ranking[0]) | (tallies[receiver] == 0), 0, jnp.maximum(room, 0))
    passed = jax.random.randint(jax.random.fold_in(own, 4), (amount // 2,), 0, 1 << 20) % (room + 1)
    tallies = tallies.at[donor].add(-passed).at[receiver].add(passed)
    items = jnp.searchsorted(jnp.cumsum(tallies), jnp.arange(rows * top), side="right").astype(jnp.int32)
    table = items.reshape(top, rows).T
    table = table[jax.random.permutation(jax.random.fold_in(own, 1), rows)]
    offset_by = jax.random.randint(jax.random.fold_in(own, 2), (rows, 1), 0, top)
    return jnp.take_along_axis(table, (jnp.arange(top)[None, :] + offset_by) % top, axis=1)


def load_shares(number_of, total, reach, lean, full):
    weights = [(1 << 20) // math.isqrt(grade ** lean) + 1 for grade in range(1, number_of + 1)]
    largest = reach if full else min(reach, max(-(-total // number_of), total * weights[0] // sum(weights)))
    least = 1 if total - largest >= number_of - 1 else 0
    given, spare = [largest] + [least] * (number_of - 1), total - largest - least * (number_of - 1)
    while spare > 0:
        candidates = [i for i in range(1, number_of) if given[i] < largest] or [i for i in range(1, number_of) if given[i] < reach]
        whole, remaining = sum([weights[i] for i in candidates]), spare
        for i in candidates:
            extra = min(reach - given[i], max(1, remaining * weights[i] // whole), spare)
            given[i] = given[i] + extra
            spare = spare - extra
    return np.array(given)


def centred(rng, dims, scale, reach, shards=(), kind=jnp.bfloat16):
    array = jax.random.normal(rng, dims, jnp.float32) * scale
    if len(shards) > 0:
        array = shard_levels(rng, dims, shards, -0.22, 0.18) * array
    return jnp.clip(array, min=-reach, max=reach).astype(kind)


def setup_inputs(seed: int = 0) -> dict:
    key_of = jax.random.split(jax.random.key(seed), 9)
    tokens = centred(key_of[0], (CLIPS, CLIP_TOK, D), 1.0, 6.0, ((0, 48), (1, 16)))
    target_kv = centred(key_of[1], (D, 2 * ATT), D ** -0.5, 0.15625, ((0, 16),))
    context_kv = centred(key_of[2], (D, 2 * ATT), D ** -0.5, 0.15625, ((0, 16),))
    query_weight = centred(key_of[3], (ATT, D), D ** -0.5, 0.15625)
    pred_hidden = centred(key_of[4], (CLIPS, CLIP_TOK, PRED), 1.0, 6.0, ((0, 48), (1, 16)))
    pred_weight = centred(key_of[5], (EXPERTS, ATT, PRED), PRED ** -0.5, 0.3125, ((0, 48),))
    target_mask = plant((jax.random.randint(key_of[6], (CLIPS, BLOCKS), 0, 4) < 3).astype(jnp.int32), jax.random.fold_in(key_of[6], 1), 0, 1)
    owners_keys = jax.random.split(jax.random.fold_in(key_of[7], 1), CLIPS * BLOCKS // BLOCKS_DEV)
    owners_turns = jax.random.permutation(jax.random.fold_in(key_of[7], 3), CLIPS * BLOCKS // BLOCKS_DEV)
    owners = jax.vmap(lambda own, number: shared_out(jax.random.fold_in(key_of[7], 2), own, number, BLOCKS_DEV, EXPERTS, 1, CAP, 2))(owners_keys, owners_turns).reshape((CLIPS, BLOCKS, 1))
    return {"tokens": tokens, "target_kv": target_kv, "context_kv": context_kv, "query_weight": query_weight, "pred_hidden": pred_hidden, "pred_weight": pred_weight, "target_mask": target_mask, "owners": owners}


keep_rate = 0.9
epsilon = 1e-05

def layer_norm(values):
    center = values - lax.optimization_barrier(jnp.mean(values, axis=-1, keepdims=True))
    variance = lax.optimization_barrier(jnp.mean(center * center, axis=-1, keepdims=True))
    return center * lax.rsqrt(variance + epsilon)

def rounded(values):
    return lax.optimization_barrier(values.astype(jnp.bfloat16)).astype(jnp.float32)

def norm_backward(upstream, normed, inputs):
    center = inputs - lax.optimization_barrier(jnp.mean(inputs, axis=-1, keepdims=True))
    variance = lax.optimization_barrier(jnp.mean(center * center, axis=-1, keepdims=True))
    inverse = lax.rsqrt(variance + epsilon)
    upstream_mean = lax.optimization_barrier(jnp.mean(upstream, axis=-1, keepdims=True))
    cross_mean = lax.optimization_barrier(jnp.mean(upstream * normed, axis=-1, keepdims=True))
    return inverse * (upstream - upstream_mean - normed * cross_mean)

def reference(tokens, target_kv, context_kv, query_weight, pred_hidden, pred_weight, target_mask, owners):
    blended = (keep_rate * target_kv.astype(jnp.float32) + (1.0 - keep_rate) * context_kv.astype(jnp.float32)).astype(jnp.bfloat16)
    width = HEADS * HEAD
    scale = 1.0 / math.sqrt(HEAD)

    def clip_targets(clip):
        length = clip.shape[0]
        normed = layer_norm(clip.astype(jnp.float32)).astype(jnp.bfloat16)
        queries = rounded(jnp.dot(normed, query_weight.T, preferred_element_type=jnp.float32))
        key_values = rounded(jnp.dot(normed, blended, preferred_element_type=jnp.float32))
        query_heads = queries.reshape(length, HEADS, HEAD)
        keys = key_values[:, :width].reshape(length, HEADS, HEAD)
        values = key_values[:, width:].reshape(length, HEADS, HEAD)
        scores = jnp.einsum('qhd,khd->hqk', query_heads, keys) * scale
        expo = jnp.exp(scores)
        denominator = lax.optimization_barrier(jnp.sum(expo, axis=-1))
        numerator = jnp.einsum('hqk,khd->qhd', rounded(expo), values)
        attended = (numerator / denominator.T[:, :, None]).reshape(length, width)
        return layer_norm(attended).astype(jnp.bfloat16)
    targets = lax.map(clip_targets, tokens)
    pred_size = pred_hidden.shape[2]
    flat_hidden = pred_hidden.reshape(-1, pred_size)
    flat_targets = targets.reshape(-1, width)
    owner_tokens = jnp.repeat(owners[:, :, 0], 2, axis=1).reshape(-1).astype(jnp.int32)
    live_tokens = jnp.repeat(target_mask, 2, axis=1).reshape(-1)
    total = flat_hidden.shape[0]
    block = math.gcd(total, 256)
    count = total // block

    def block_grad(pieces):
        hidden, target_rows, owner_ids, live = pieces
        inputs = hidden.astype(jnp.float32)
        normed = layer_norm(inputs)
        experts = pred_weight[owner_ids].astype(jnp.float32)
        prediction = jnp.einsum('tp,tap->ta', rounded(normed), experts)
        residual = prediction - target_rows.astype(jnp.float32)
        upstream = jnp.einsum('ta,tap->tp', rounded(residual), experts)
        grad = norm_backward(upstream, normed, inputs)
        return (grad * live[:, None].astype(jnp.float32)).astype(jnp.bfloat16)
    grads = lax.map(block_grad, (flat_hidden.reshape(count, block, pred_size), flat_targets.reshape(count, block, width), owner_tokens.reshape(count, block), live_tokens.reshape(count, block)))
    return (blended, targets, grads.reshape(pred_hidden.shape))
```

```python
import math

import jax
import jax.numpy as jnp
from jax import lax
from jax.experimental import pallas as pl
from jax.experimental.pallas import tpu as pltpu
from jax.sharding import PartitionSpec as P

HEAD = 64
HEADS = 11
SEQ = 16
GRP = 48
ROWS = 128
PAIRS = 64
D = 1408
ATT = 704
PRED = 384
SHARD = 88
LO = 768
SLAB = 4
SLOTS = GRP * SLAB

keep_rate = 0.9
epsilon = 1e-05

F32 = jnp.float32
BF16 = jnp.bfloat16


def normalize(values):
    center = values - jnp.mean(values, axis=-1, keepdims=True)
    variance = jnp.mean(center * center, axis=-1, keepdims=True)
    inverse = lax.rsqrt(variance + epsilon)
    return center * inverse, inverse


def dot(a, b):
    return jnp.dot(a, b, preferred_element_type=F32)


def dot_t(a, b):
    return lax.dot_general(a, b, (((1,), (1,)), ((), ())), preferred_element_type=F32)


def iota(shape, axis):
    return lax.broadcasted_iota(jnp.int32, shape, axis)


def slot_rows(own_col, mask_row):
    shape = (PAIRS, PAIRS)
    down, across = iota(shape, 0), iota(shape, 1)
    same = down == across
    own_down = jnp.broadcast_to(own_col, shape)
    live_across = jnp.broadcast_to(mask_row, shape)
    own_across = jnp.broadcast_to(
        jnp.sum(jnp.where(same, own_down, 0.0), axis=0, keepdims=True), shape
    )
    live_down = jnp.broadcast_to(
        jnp.sum(jnp.where(same, live_across, 0.0), axis=1, keepdims=True), shape
    )
    equal = own_down == own_across
    rank_row = jnp.sum(
        jnp.where(equal & (down < across), live_down, 0.0), axis=0, keepdims=True
    )
    rank_col = jnp.sum(
        jnp.where(equal & (across < down), live_across, 0.0), axis=1, keepdims=True
    )
    slot_row = jnp.where(mask_row > 0.5, own_across[:1] * 2.0 + rank_row, -1.0)
    slot_col = jnp.where(live_down[:, :1] > 0.5, own_col * 2.0 + rank_col, -1.0)
    shape = (PAIRS, ROWS)
    token_row = jnp.sum(
        jnp.where(
            iota(shape, 0) == lax.shift_right_logical(iota(shape, 1), 1),
            jnp.broadcast_to(slot_col, shape),
            0.0,
        ),
        axis=0,
        keepdims=True,
    )
    shape = (ROWS, PAIRS)
    token_col = jnp.sum(
        jnp.where(
            lax.shift_right_logical(iota(shape, 0), 1) == iota(shape, 1),
            jnp.broadcast_to(slot_row, shape),
            0.0,
        ),
        axis=1,
        keepdims=True,
    )
    return token_row, token_col


def kernel(
    tok_ref,
    tkv_ref,
    ckv_ref,
    qw_ref,
    hid_ref,
    pw_ref,
    mask_ref,
    own_ref,
    nkv_ref,
    tgt_ref,
    pg_ref,
    wbuf,
    chunks,
    acc,
    queries,
    head_out,
    head_in,
    values_one,
    att_out,
    att_in,
    spread,
    gather,
    hid_out,
    hid_in,
    tgt_out,
    tgt_in,
    grad_out,
    grad_in,
    predicted,
    w_send,
    w_recv,
    head_send,
    head_recv,
    att_send,
    att_recv,
    hid_send,
    hid_recv,
    tgt_send,
    tgt_recv,
    grad_send,
    grad_recv,
):
    me = lax.axis_index("seq")
    mine = lax.axis_index("grp")
    core = lax.rem(me, 2)
    x = lax.rem(me // 2, 4)
    y = me // 8
    z = mine // 4
    yh = lax.rem(mine, 4)

    def place(xx, yy, cc):
        return (lax.rem(xx, 4) + yy * 4) * 2 + cc

    right, left, far = place(x + 1, y, core), place(x + 3, y, core), place(x + 2, y, core)
    across = place(x, 1 - y, core)
    right_p, left_p, far_p = (
        place(x + 1, 1 - y, core),
        place(x + 3, 1 - y, core),
        place(x + 2, 1 - y, core),
    )
    twin = place(x, y, 1 - core)
    up_grp = z * 4 + lax.rem(yh + y, 4)
    down_grp = z * 4 + lax.rem(yh + 3 * (1 - y), 4)
    other_grp = z * 4 + lax.rem(yh + 3 + 2 * y, 4)

    barrier = pltpu.get_barrier_semaphore()

    @pl.loop(1, SEQ)
    def _(k):
        pl.semaphore_signal(barrier, inc=1, device_id={"seq": lax.rem(me + k, SEQ), "grp": mine})

    @pl.loop(1, GRP)
    def _(k):
        pl.semaphore_signal(barrier, inc=1, device_id={"seq": me, "grp": lax.rem(mine + k, GRP)})

    pl.semaphore_signal(barrier, inc=1, device_id={"seq": across, "grp": other_grp})

    blended = (
        keep_rate * tkv_ref[...].astype(F32) + (1.0 - keep_rate) * ckv_ref[...].astype(F32)
    ).astype(BF16)
    nkv_ref[...] = blended
    wbuf[me] = blended
    pl.semaphore_wait(barrier, SEQ - 1 + GRP - 1 + 1)

    started = []

    def push(ref, slot, seq, grp):
        copy = pltpu.make_async_remote_copy(
            src_ref=ref,
            dst_ref=ref,
            send_sem=w_send.at[len(started)],
            recv_sem=w_recv.at[slot],
            device_id={"seq": seq, "grp": grp},
        )
        copy.start()
        started.append(copy)

    def arrive(ref, slot):
        pltpu.make_async_remote_copy(
            src_ref=ref,
            dst_ref=ref,
            send_sem=w_send.at[0],
            recv_sem=w_recv.at[slot],
            device_id={"seq": twin, "grp": mine},
        ).wait_recv()

    def lo(block):
        return wbuf.at[block, :, pl.ds(0, LO)]

    def hi(block):
        return wbuf.at[block, :, pl.ds(LO, D - LO)]

    push(wbuf.at[me], 0, right, mine)
    push(wbuf.at[me], 1, left, mine)
    push(lo(me), 2, across, up_grp)
    push(hi(me), 3, across, down_grp)
    push(wbuf.at[me], 10, twin, mine)

    normed = normalize(tok_ref[...].astype(F32))[0]
    for s in range(SEQ):
        chunks[s] = normed[:, s * SHARD : (s + 1) * SHARD].astype(BF16)
    queries[...] = dot_t(normed.astype(BF16), qw_ref[...])
    token_row, token_col = slot_rows(
        own_ref[...].astype(F32), mask_ref[...].astype(F32)
    )
    shape = (SLOTS, ROWS)
    spread[...] = jnp.where(
        (
            lax.shift_right_logical(iota(shape, 0), 1)
            == jnp.broadcast_to(token_row, shape).astype(jnp.int32)
        )
        & (lax.bitwise_and(iota(shape, 0), 1) == lax.bitwise_and(iota(shape, 1), 1)),
        1.0,
        0.0,
    ).astype(BF16)
    shape = (ROWS, SLOTS)
    gather[...] = jnp.where(
        (
            lax.shift_right_logical(iota(shape, 1), 1)
            == jnp.broadcast_to(token_col, shape).astype(jnp.int32)
        )
        & (lax.bitwise_and(iota(shape, 0), 1) == lax.bitwise_and(iota(shape, 1), 1)),
        1.0,
        0.0,
    ).astype(BF16)

    def to_slabs(rows, out):
        out[...] = rows.reshape(GRP, SLAB, rows.shape[1]).astype(BF16)

    to_slabs(dot(spread[...], hid_ref[...]), hid_out)

    def term(block):
        return dot(chunks[block], wbuf[block])

    acc[...] = term(me)
    arrive(wbuf.at[left], 0)
    push(lo(left), 4, right, mine)
    push(wbuf.at[left], 6, across, up_grp)
    push(wbuf.at[left], 11, twin, mine)
    arrive(wbuf.at[right], 1)
    push(hi(right), 5, left, mine)
    push(wbuf.at[right], 7, across, down_grp)
    push(wbuf.at[right], 12, twin, mine)
    arrive(lo(across), 2)
    arrive(hi(across), 3)
    push(wbuf.at[across], 13, twin, mine)
    twin_of = 1 - 2 * core
    arrive(wbuf.at[twin], 10)
    acc[...] += term(left) + term(right)
    acc[...] += term(across) + term(twin)
    arrive(lo(far), 4)
    push(lo(far), 8, across, up_grp)
    arrive(hi(far), 5)
    push(hi(far), 9, across, down_grp)
    push(wbuf.at[far], 14, twin, mine)
    arrive(wbuf.at[left + twin_of], 11)
    arrive(wbuf.at[right + twin_of], 12)
    arrive(wbuf.at[across + twin_of], 13)
    acc[...] += term(far) + term(left + twin_of)
    acc[...] += term(right + twin_of) + term(across + twin_of)
    arrive(wbuf.at[left_p], 6)
    push(wbuf.at[left_p], 15, twin, mine)
    arrive(wbuf.at[right_p], 7)
    push(wbuf.at[right_p], 16, twin, mine)
    arrive(wbuf.at[far + twin_of], 14)
    acc[...] += term(left_p) + term(right_p) + term(far + twin_of)
    arrive(lo(far_p), 8)
    arrive(hi(far_p), 9)
    push(wbuf.at[far_p], 17, twin, mine)
    acc[...] += term(far_p)
    arrive(wbuf.at[left_p + twin_of], 15)
    arrive(wbuf.at[right_p + twin_of], 16)
    acc[...] += term(left_p + twin_of) + term(right_p + twin_of)
    arrive(wbuf.at[far_p + twin_of], 17)
    acc[...] += term(far_p + twin_of)

    def head_place(h):
        return 2 * h if h < 8 else 1 + 4 * (h - 8)

    for h in range(HEADS):
        k_h = acc[:, h * HEAD : (h + 1) * HEAD]
        v_h = acc[:, ATT + h * HEAD : ATT + (h + 1) * HEAD]
        q_h = queries[:, h * HEAD : (h + 1) * HEAD]
        head_out[h, :ROWS] = jnp.concatenate([v_h, k_h], axis=1).astype(BF16)
        head_out[h, ROWS:] = jnp.concatenate([q_h[PAIRS:], q_h[:PAIRS]], axis=1).astype(BF16)
        to = head_place(h)

        @pl.when(me != to)
        def _():
            pltpu.make_async_remote_copy(
                src_ref=head_out.at[h],
                dst_ref=head_in.at[me],
                send_sem=head_send.at[h],
                recv_sem=head_recv.at[me],
                device_id={"seq": to, "grp": mine},
            ).start()

        @pl.when(me == to)
        def _():
            pltpu.make_async_copy(head_out.at[h], head_in.at[me], head_recv.at[me]).start()

    def exchange(out, into, send, recv):
        @pl.loop(1, GRP)
        def _(k):
            to = lax.rem(mine + k, GRP)
            pltpu.make_async_remote_copy(
                src_ref=out.at[to],
                dst_ref=into.at[mine],
                send_sem=send.at[to],
                recv_sem=recv.at[mine],
                device_id={"seq": me, "grp": to},
            ).start()

        pltpu.make_async_copy(out.at[mine], into.at[mine], recv.at[mine]).start()

    def received(out, into, send, recv):
        @pl.loop(0, GRP)
        def _(k):
            pltpu.make_async_copy(out.at[k], into.at[k], recv.at[k]).wait()

    def sent(out, into, send, recv):
        @pl.loop(1, GRP)
        def _(k):
            to = lax.rem(mine + k, GRP)
            pltpu.make_async_copy(out.at[to], into.at[to], send.at[to]).wait()

    hid_way = (hid_out, hid_in, hid_send, hid_recv)
    tgt_way = (tgt_out, tgt_in, tgt_send, tgt_recv)
    grad_way = (grad_out, grad_in, grad_send, grad_recv)
    exchange(*hid_way)

    even = lax.rem(me, 2) == 0
    is_head = even | ((lax.rem(me, 4) == 1) & (me < 12))
    my_head = jnp.where(even, me // 2, 8 + me // 4)

    @pl.when(is_head)
    def _():
        @pl.loop(0, SEQ)
        def _(t):
            pltpu.make_async_copy(head_out.at[0], head_in.at[t], head_recv.at[t]).wait()

        lane = iota((ROWS, 2 * HEAD), 1)

        @pl.loop(0, SEQ)
        def _(t):
            block = head_in[t, :ROWS].astype(F32)
            values_one[t] = jnp.where(lane < HEAD, block, 1.0).astype(BF16)

        rate = math.log2(math.e) / math.sqrt(HEAD)

        @pl.loop(0, SEQ // 2)
        def _(i):
            zero = jnp.zeros((PAIRS, HEAD), BF16)
            parts = []
            for j in range(2):
                packed = head_in[2 * i + j, ROWS:]
                parts.append(jnp.concatenate([zero, packed[:, HEAD:]], axis=1))
                parts.append(jnp.concatenate([zero, packed[:, :HEAD]], axis=1))
            q = jnp.concatenate(parts, axis=0)
            kv = head_in[:, :ROWS].reshape(SEQ * ROWS, 2 * HEAD)
            score = dot_t(q, kv)
            expo = jnp.exp2(score * rate).astype(BF16)
            added = dot(expo, values_one[...].reshape(SEQ * ROWS, 2 * HEAD))
            attended = added[:, :HEAD] / added[:, HEAD:]
            for j in range(2):
                rows = attended[j * ROWS : (j + 1) * ROWS]
                to = 2 * i + j
                att_out[to] = jnp.concatenate([rows[:PAIRS], rows[PAIRS:]], axis=1).astype(BF16)

                @pl.when(me != to)
                def _():
                    pltpu.make_async_remote_copy(
                        src_ref=att_out.at[to],
                        dst_ref=att_in.at[my_head],
                        send_sem=att_send.at[to],
                        recv_sem=att_recv.at[my_head],
                        device_id={"seq": to, "grp": mine},
                    ).start()

                @pl.when(me == to)
                def _():
                    pltpu.make_async_copy(
                        att_out.at[to], att_in.at[my_head], att_recv.at[my_head]
                    ).start()

    @pl.loop(0, HEADS)
    def _(h):
        pltpu.make_async_copy(att_out.at[0], att_in.at[h], att_recv.at[h]).wait()

    top = jnp.concatenate([att_in[h][:, :HEAD].astype(F32) for h in range(HEADS)], axis=1)
    low = jnp.concatenate([att_in[h][:, HEAD:].astype(F32) for h in range(HEADS)], axis=1)
    attended = jnp.concatenate([top, low], axis=0)
    targets = normalize(attended)[0].astype(BF16)
    tgt_ref[...] = targets
    to_slabs(dot(spread[...], targets), tgt_out)
    exchange(*tgt_way)

    def from_slabs(into):
        return into[...].reshape(SLOTS, into.shape[2])

    received(*hid_way)
    inputs = from_slabs(hid_in).astype(F32)
    normed_h, inverse = normalize(inputs)
    predicted[...] = dot_t(normed_h.astype(BF16), pw_ref[...])
    received(*tgt_way)
    residual = (predicted[...] - from_slabs(tgt_in).astype(F32)).astype(BF16)
    upstream = dot(residual, pw_ref[...])
    upstream_mean = jnp.mean(upstream, axis=-1, keepdims=True)
    cross_mean = jnp.mean(upstream * normed_h, axis=-1, keepdims=True)
    to_slabs(inverse * (upstream - upstream_mean - normed_h * cross_mean), grad_out)
    exchange(*grad_way)
    received(*grad_way)
    pg_ref[...] = dot(gather[...], from_slabs(grad_in)).astype(BF16)

    for copy in started:
        copy.wait_send()
    for h in range(HEADS):

        @pl.when(me != head_place(h))
        def _():
            pltpu.make_async_copy(head_out.at[h], head_in.at[0], head_send.at[h]).wait()

    @pl.when(is_head)
    def _():
        @pl.loop(1, SEQ)
        def _(k):
            to = lax.rem(me + k, SEQ)
            pltpu.make_async_copy(att_out.at[to], att_in.at[0], att_send.at[to]).wait()

    sent(*hid_way)
    sent(*tgt_way)
    sent(*grad_way)


def shards(
    tokens, target_kv, context_kv, query_weight, pred_hidden, pred_weight, target_mask, owners
):
    vmem = pl.BlockSpec(memory_space=pltpu.VMEM)
    dma = pltpu.SemaphoreType.DMA
    new_kv, targets, pred_grad = pl.pallas_call(
        kernel,
        out_shape=(
            jax.ShapeDtypeStruct((SHARD, D), BF16),
            jax.ShapeDtypeStruct((ROWS, ATT), BF16),
            jax.ShapeDtypeStruct((ROWS, PRED), BF16),
        ),
        in_specs=[vmem] * 8,
        out_specs=(vmem,) * 3,
        scratch_shapes=[
            pltpu.VMEM((SEQ, SHARD, D), BF16),
            pltpu.VMEM((SEQ, ROWS, SHARD), BF16),
            pltpu.VMEM((ROWS, D), F32),
            pltpu.VMEM((ROWS, ATT), F32),
            pltpu.VMEM((HEADS, ROWS + PAIRS, 2 * HEAD), BF16),
            pltpu.VMEM((SEQ, ROWS + PAIRS, 2 * HEAD), BF16),
            pltpu.VMEM((SEQ, ROWS, 2 * HEAD), BF16),
            pltpu.VMEM((SEQ, PAIRS, 2 * HEAD), BF16),
            pltpu.VMEM((HEADS, PAIRS, 2 * HEAD), BF16),
            pltpu.VMEM((SLOTS, ROWS), BF16),
            pltpu.VMEM((ROWS, SLOTS), BF16),
            pltpu.VMEM((GRP, SLAB, PRED), BF16),
            pltpu.VMEM((GRP, SLAB, PRED), BF16),
            pltpu.VMEM((GRP, SLAB, ATT), BF16),
            pltpu.VMEM((GRP, SLAB, ATT), BF16),
            pltpu.VMEM((GRP, SLAB, PRED), BF16),
            pltpu.VMEM((GRP, SLAB, PRED), BF16),
            pltpu.VMEM((SLOTS, ATT), F32),
            dma((24,)),
            dma((18,)),
            dma((HEADS,)),
            dma((SEQ,)),
            dma((SEQ,)),
            dma((HEADS,)),
            dma((GRP,)),
            dma((GRP,)),
            dma((GRP,)),
            dma((GRP,)),
            dma((GRP,)),
            dma((GRP,)),
        ],
        compiler_params=pltpu.CompilerParams(
            collective_id=0, has_side_effects=True, vmem_limit_bytes=48 * 1024 * 1024
        ),
        cost_estimate=pl.CostEstimate(
            flops=2_000_000_000, bytes_accessed=5_000_000, transcendentals=3_000_000
        ),
        name="attend_and_route",
    )(
        tokens[0],
        target_kv,
        context_kv,
        query_weight,
        pred_hidden[0],
        pred_weight[0],
        target_mask,
        owners[0],
    )
    return new_kv, targets[None], pred_grad[None]


def solution(mesh):
    placed = (
        P("grp", "seq", None),
        P("seq", None),
        P("seq", None),
        P(),
        P("grp", "seq", None),
        P("grp", None, None),
        P("grp", "seq"),
        P("grp", "seq", None),
    )
    return jax.shard_map(
        shards,
        mesh=mesh,
        in_specs=placed,
        out_specs=(P("seq", None), P("grp", "seq", None), P("grp", "seq", None)),
        check_vma=False,
    )
```

```python
import math

import jax
import jax.numpy as jnp
from jax import lax
from jax.experimental import pallas as pl
from jax.experimental.pallas import tpu as pltpu
from jax.sharding import PartitionSpec as P

HEAD = 64
HEADS = 11
SEQ = 16
GRP = 48
ROWS = 128
PAIRS = 64
D = 1408
ATT = 704
PRED = 384
SHARD = 88
LO = 768
SLAB = 4
SLOTS = GRP * SLAB

keep_rate = 0.9
epsilon = 1e-05

F32 = jnp.float32
BF16 = jnp.bfloat16


def normalize(values):
    center = values - jnp.mean(values, axis=-1, keepdims=True)
    variance = jnp.mean(center * center, axis=-1, keepdims=True)
    inverse = lax.rsqrt(variance + epsilon)
    return center * inverse, inverse


def dot(a, b):
    return jnp.dot(a, b, preferred_element_type=F32)


def dot_t(a, b):
    return lax.dot_general(a, b, (((1,), (1,)), ((), ())), preferred_element_type=F32)


def iota(shape, axis):
    return lax.broadcasted_iota(jnp.int32, shape, axis)


def slot_rows(own_row, mask_row):
    shape = (PAIRS, PAIRS)
    down, across = iota(shape, 0), iota(shape, 1)
    same = down == across

    def turned(row):
        return jnp.broadcast_to(
            jnp.sum(jnp.where(same, row, 0.0), axis=1, keepdims=True), shape
        )

    own_across = jnp.broadcast_to(own_row, shape)
    live_across = jnp.broadcast_to(mask_row, shape)
    own_down, live_down = turned(own_across), turned(live_across)
    equal = own_down == own_across
    rank_row = jnp.sum(
        jnp.where(equal & (down < across), live_down, 0.0), axis=0, keepdims=True
    )
    rank_col = jnp.sum(
        jnp.where(equal & (across < down), live_across, 0.0), axis=1, keepdims=True
    )
    slot_row = jnp.where(mask_row > 0.5, own_across[:1] * 2.0 + rank_row, -1.0)
    slot_col = jnp.where(live_down[:, :1] > 0.5, own_down[:, :1] * 2.0 + rank_col, -1.0)
    shape = (PAIRS, ROWS)
    token_row = jnp.sum(
        jnp.where(
            iota(shape, 0) == lax.shift_right_logical(iota(shape, 1), 1),
            jnp.broadcast_to(slot_col, shape),
            0.0,
        ),
        axis=0,
        keepdims=True,
    )
    shape = (ROWS, PAIRS)
    token_col = jnp.sum(
        jnp.where(
            lax.shift_right_logical(iota(shape, 0), 1) == iota(shape, 1),
            jnp.broadcast_to(slot_row, shape),
            0.0,
        ),
        axis=1,
        keepdims=True,
    )
    return token_row, token_col


def dispatch_tables(own_row, mask_row):
    token_row, token_col = slot_rows(own_row, mask_row)
    shape = (SLOTS, ROWS)
    spread = jnp.where(
        (
            lax.shift_right_logical(iota(shape, 0), 1)
            == jnp.broadcast_to(token_row, shape).astype(jnp.int32)
        )
        & (lax.bitwise_and(iota(shape, 0), 1) == lax.bitwise_and(iota(shape, 1), 1)),
        1.0,
        0.0,
    ).astype(BF16)
    shape = (ROWS, SLOTS)
    gather = jnp.where(
        (
            lax.shift_right_logical(iota(shape, 1), 1)
            == jnp.broadcast_to(token_col, shape).astype(jnp.int32)
        )
        & (lax.bitwise_and(iota(shape, 0), 1) == lax.bitwise_and(iota(shape, 1), 1)),
        1.0,
        0.0,
    ).astype(BF16)
    return spread, gather


def kernel(
    tok_hbm,
    tkv_hbm,
    ckv_hbm,
    qw_hbm,
    hid_hbm,
    pw_hbm,
    mask_hbm,
    own_hbm,
    nkv_ref,
    tgt_ref,
    pg_ref,
    tok_ref,
    tkv_ref,
    ckv_ref,
    qw_ref,
    hid_ref,
    pw_ref,
    mask_ref,
    own_ref,
    load_sem,
    wbuf,
    chunks,
    acc,
    queries,
    head_out,
    head_in,
    values_one,
    att_out,
    att_in,
    spread,
    gather,
    hid_out,
    hid_in,
    tgt_out,
    tgt_in,
    grad_out,
    grad_in,
    predicted,
    normed_h,
    inverses,
    w_send,
    w_recv,
    head_send,
    head_recv,
    att_send,
    att_recv,
    hid_send,
    hid_recv,
    tgt_send,
    tgt_recv,
    grad_send,
    grad_recv,
):
    loads = [
        pltpu.make_async_copy(src, dst, load_sem.at[i])
        for i, (src, dst) in enumerate(
            (
                (tkv_hbm, tkv_ref),
                (ckv_hbm, ckv_ref),
                (tok_hbm, tok_ref),
                (qw_hbm, qw_ref),
                (mask_hbm, mask_ref),
                (own_hbm, own_ref),
                (hid_hbm, hid_ref),
                (pw_hbm, pw_ref),
            )
        )
    ]
    for load in loads:
        load.start()
    me = lax.axis_index("seq")
    mine = lax.axis_index("grp")
    core = lax.rem(me, 2)
    x = lax.rem(me // 2, 4)
    y = me // 8
    z = mine // 4
    yh = lax.rem(mine, 4)

    def place(xx, yy, cc):
        return (lax.rem(xx, 4) + yy * 4) * 2 + cc

    right, left, far = place(x + 1, y, core), place(x + 3, y, core), place(x + 2, y, core)
    across = place(x, 1 - y, core)
    right_p, left_p, far_p = (
        place(x + 1, 1 - y, core),
        place(x + 3, 1 - y, core),
        place(x + 2, 1 - y, core),
    )
    twin = place(x, y, 1 - core)
    up_grp = z * 4 + lax.rem(yh + y, 4)
    down_grp = z * 4 + lax.rem(yh + 3 * (1 - y), 4)
    other_grp = z * 4 + lax.rem(yh + 3 + 2 * y, 4)

    barrier = pltpu.get_barrier_semaphore()

    @pl.loop(1, SEQ)
    def _(k):
        pl.semaphore_signal(barrier, inc=1, device_id={"seq": lax.rem(me + k, SEQ), "grp": mine})

    @pl.loop(1, GRP)
    def _(k):
        pl.semaphore_signal(barrier, inc=1, device_id={"seq": me, "grp": lax.rem(mine + k, GRP)})

    pl.semaphore_signal(barrier, inc=1, device_id={"seq": across, "grp": other_grp})

    loads[0].wait()
    loads[1].wait()
    blended = (
        keep_rate * tkv_ref[...].astype(F32) + (1.0 - keep_rate) * ckv_ref[...].astype(F32)
    ).astype(BF16)
    nkv_ref[...] = blended
    wbuf[me] = blended
    pl.semaphore_wait(barrier, SEQ - 1 + GRP - 1 + 1)

    started = []

    def push(ref, slot, seq, grp):
        copy = pltpu.make_async_remote_copy(
            src_ref=ref,
            dst_ref=ref,
            send_sem=w_send.at[len(started)],
            recv_sem=w_recv.at[slot],
            device_id={"seq": seq, "grp": grp},
        )
        copy.start()
        started.append(copy)

    def arrive(ref, slot):
        pltpu.make_async_remote_copy(
            src_ref=ref,
            dst_ref=ref,
            send_sem=w_send.at[0],
            recv_sem=w_recv.at[slot],
            device_id={"seq": twin, "grp": mine},
        ).wait_recv()

    def lo(block):
        return wbuf.at[block, :, pl.ds(0, LO)]

    def hi(block):
        return wbuf.at[block, :, pl.ds(LO, D - LO)]

    push(lo(me), 0, right, mine)
    push(hi(me), 3, left, mine)
    push(lo(me), 4, across, up_grp)
    push(hi(me), 5, across, down_grp)
    push(hi(me), 1, right, mine)
    push(lo(me), 2, left, mine)
    push(wbuf.at[me], 14, twin, mine)

    loads[2].wait()
    normed = normalize(tok_ref[...].astype(F32))[0]
    for s in range(SEQ):
        chunks[s] = normed[:, s * SHARD : (s + 1) * SHARD].astype(BF16)
    normed_b = normed.astype(BF16)
    twin_of = 1 - 2 * core

    def term(block):
        return dot(chunks[block], wbuf[block])

    arrive(lo(left), 0)
    push(lo(left), 6, right, mine)
    push(lo(left), 8, across, up_grp)
    arrive(hi(right), 3)
    push(hi(right), 7, left, mine)
    push(hi(right), 11, across, down_grp)
    arrive(lo(across), 4)
    arrive(hi(across), 5)
    push(wbuf.at[across], 17, twin, mine)
    loads[3].wait()
    queries[...] = dot_t(normed_b, qw_ref[...])
    arrive(hi(left), 1)
    push(hi(left), 9, across, up_grp)
    push(wbuf.at[left], 15, twin, mine)
    arrive(lo(right), 2)
    push(lo(right), 10, across, down_grp)
    push(wbuf.at[right], 16, twin, mine)
    arrive(wbuf.at[twin], 14)
    acc[...] = term(me) + term(twin) + term(across)
    arrive(lo(left_p), 8)
    push(lo(left_p), 12, right, mine)
    arrive(hi(right_p), 11)
    push(hi(right_p), 13, left, mine)
    acc[...] += term(left) + term(right)
    arrive(lo(far), 6)
    arrive(hi(far), 7)
    push(wbuf.at[far], 18, twin, mine)
    arrive(wbuf.at[left + twin_of], 15)
    arrive(wbuf.at[right + twin_of], 16)
    arrive(wbuf.at[across + twin_of], 17)
    acc[...] += term(far) + term(left + twin_of) + term(right + twin_of) + term(across + twin_of)
    arrive(hi(left_p), 9)
    push(wbuf.at[left_p], 19, twin, mine)
    arrive(lo(right_p), 10)
    push(wbuf.at[right_p], 20, twin, mine)
    arrive(wbuf.at[far + twin_of], 18)
    acc[...] += term(left_p) + term(right_p) + term(far + twin_of)
    for load in loads[4:]:
        load.wait()
    spread[...], gather[...] = dispatch_tables(
        own_ref[...].astype(F32), mask_ref[...].astype(F32)
    )

    def to_slabs(rows):
        return rows.reshape(rows.shape[0] // SLAB, SLAB, rows.shape[1]).astype(BF16)

    hid_out[...] = to_slabs(dot(spread[...], hid_ref[...]))
    arrive(wbuf.at[left_p + twin_of], 19)
    arrive(wbuf.at[right_p + twin_of], 20)
    acc[...] += term(left_p + twin_of) + term(right_p + twin_of)
    arrive(lo(far_p), 12)
    push(lo(far_p), 21, twin, mine)
    arrive(hi(far_p), 13)
    push(hi(far_p), 22, twin, mine)
    acc[...] += term(far_p)
    arrive(lo(far_p + twin_of), 21)
    arrive(hi(far_p + twin_of), 22)
    acc[...] += term(far_p + twin_of)

    def head_place(h):
        return 2 * h if h < 8 else 1 + 4 * (h - 8)

    for h in range(HEADS):
        k_h = acc[:, h * HEAD : (h + 1) * HEAD]
        v_h = acc[:, ATT + h * HEAD : ATT + (h + 1) * HEAD]
        q_h = queries[:, h * HEAD : (h + 1) * HEAD]
        head_out[h, :ROWS] = jnp.concatenate([v_h, k_h], axis=1).astype(BF16)
        head_out[h, ROWS:] = jnp.concatenate([q_h[PAIRS:], q_h[:PAIRS]], axis=1).astype(BF16)
        to = head_place(h)

        @pl.when(me != to)
        def _():
            pltpu.make_async_remote_copy(
                src_ref=head_out.at[h],
                dst_ref=head_in.at[me],
                send_sem=head_send.at[h],
                recv_sem=head_recv.at[me],
                device_id={"seq": to, "grp": mine},
            ).start()

        @pl.when(me == to)
        def _():
            pltpu.make_async_copy(head_out.at[h], head_in.at[me], head_recv.at[me]).start()

    def outward(way, n):
        out, into, send, recv = way
        m = n // 4
        dz = GRP // 8 + (m + 1) // 2 * (1 - 2 * lax.rem(m, 2))
        to = lax.rem(z + dz, GRP // 4) * 4 + lax.rem(n, 4)
        slot = (GRP // 4 - dz) * 4 + yh
        pltpu.make_async_remote_copy(
            src_ref=out.at[to],
            dst_ref=into.at[slot],
            send_sem=send.at[n],
            recv_sem=recv.at[slot],
            device_id={"seq": me, "grp": to},
        ).start()

    def outward_near(way):
        out, into, send, recv = way

        @pl.loop(1, 4)
        def _(k):
            to = z * 4 + lax.rem(yh + k, 4)
            pltpu.make_async_remote_copy(
                src_ref=out.at[to],
                dst_ref=into.at[yh],
                send_sem=send.at[GRP - 5 + k],
                recv_sem=recv.at[yh],
                device_id={"seq": me, "grp": to},
            ).start()

        pltpu.make_async_copy(out.at[mine], into.at[yh], recv.at[yh]).start()

    def exchange(way):
        @pl.loop(0, GRP - 4)
        def _(n):
            outward(way, n)

        outward_near(way)

    def received(way, first, last):
        out, into, send, recv = way

        @pl.loop(first, last)
        def _(k):
            pltpu.make_async_copy(out.at[k], into.at[k], recv.at[k]).wait()

    def sent(way, first, last):
        out, into, send, recv = way

        @pl.loop(first, last)
        def _(k):
            pltpu.make_async_copy(out.at[k], into.at[k], send.at[k]).wait()

    def homeward(first, last):
        @pl.loop(first, last)
        def _(j):
            to = lax.rem(z + j // 4, GRP // 4) * 4 + lax.rem(j, 4)
            pltpu.make_async_remote_copy(
                src_ref=grad_out.at[j],
                dst_ref=grad_in.at[mine],
                send_sem=grad_send.at[j],
                recv_sem=grad_recv.at[mine],
                device_id={"seq": me, "grp": to},
            ).start()

    def homeward_near():
        @pl.loop(1, 4)
        def _(k):
            j = lax.rem(yh + k, 4)
            pltpu.make_async_remote_copy(
                src_ref=grad_out.at[j],
                dst_ref=grad_in.at[mine],
                send_sem=grad_send.at[j],
                recv_sem=grad_recv.at[mine],
                device_id={"seq": me, "grp": z * 4 + j},
            ).start()

        pltpu.make_async_copy(grad_out.at[yh], grad_in.at[mine], grad_recv.at[mine]).start()

    hid_way = (hid_out, hid_in, hid_send, hid_recv)
    tgt_way = (tgt_out, tgt_in, tgt_send, tgt_recv)
    grad_way = (grad_out, grad_in, grad_send, grad_recv)

    even = lax.rem(me, 2) == 0
    is_head = even | ((lax.rem(me, 4) == 1) & (me < 12))
    my_head = jnp.where(even, me // 2, 8 + me // 4)

    @pl.when(is_head)
    def _():
        @pl.loop(0, SEQ)
        def _(t):
            pltpu.make_async_copy(head_out.at[0], head_in.at[t], head_recv.at[t]).wait()

        lane = iota((ROWS, 2 * HEAD), 1)

        @pl.loop(0, SEQ)
        def _(t):
            block = head_in[t, :ROWS].astype(F32)
            values_one[t] = jnp.where(lane < HEAD, block, 1.0).astype(BF16)

        rate = math.log2(math.e) / math.sqrt(HEAD)

        @pl.loop(0, SEQ // 2)
        def _(i):
            zero = jnp.zeros((PAIRS, HEAD), BF16)
            parts = []
            for j in range(2):
                packed = head_in[2 * i + j, ROWS:]
                parts.append(jnp.concatenate([zero, packed[:, HEAD:]], axis=1))
                parts.append(jnp.concatenate([zero, packed[:, :HEAD]], axis=1))
            q = jnp.concatenate(parts, axis=0)
            for j in range(5):
                outward(hid_way, 5 * i + j)
            kv = head_in[:, :ROWS].reshape(SEQ * ROWS, 2 * HEAD)
            score = dot_t(q, kv)
            expo = jnp.exp2(score * rate).astype(BF16)
            added = dot(expo, values_one[...].reshape(SEQ * ROWS, 2 * HEAD))
            attended = added[:, :HEAD] / added[:, HEAD:]
            for j in range(2):
                rows = attended[j * ROWS : (j + 1) * ROWS]
                to = 2 * i + j
                att_out[to] = jnp.concatenate([rows[:PAIRS], rows[PAIRS:]], axis=1).astype(BF16)

                @pl.when(me != to)
                def _():
                    pltpu.make_async_remote_copy(
                        src_ref=att_out.at[to],
                        dst_ref=att_in.at[my_head],
                        send_sem=att_send.at[to],
                        recv_sem=att_recv.at[my_head],
                        device_id={"seq": to, "grp": mine},
                    ).start()

                @pl.when(me == to)
                def _():
                    pltpu.make_async_copy(
                        att_out.at[to], att_in.at[my_head], att_recv.at[my_head]
                    ).start()

        @pl.loop(5 * SEQ // 2, GRP - 4)
        def _(n):
            outward(hid_way, n)

        outward_near(hid_way)

    @pl.when(jnp.logical_not(is_head))
    def _():
        exchange(hid_way)

    @pl.loop(0, HEADS)
    def _(h):
        pltpu.make_async_copy(att_out.at[0], att_in.at[h], att_recv.at[h]).wait()

    top = jnp.concatenate([att_in[h][:, :HEAD].astype(F32) for h in range(HEADS)], axis=1)
    low = jnp.concatenate([att_in[h][:, HEAD:].astype(F32) for h in range(HEADS)], axis=1)
    attended = jnp.concatenate([top, low], axis=0)
    targets = normalize(attended)[0]
    tgt_out[...] = to_slabs(dot(spread[...], targets.astype(BF16)))
    exchange(tgt_way)
    tgt_ref[...] = targets.T.astype(BF16)

    received(hid_way, 0, GRP)
    owned, inverse = normalize(hid_in[...].reshape(SLOTS, PRED).astype(F32))
    normed_h[...] = owned
    inverses[...] = inverse
    predicted[...] = dot_t(owned.astype(BF16), pw_ref[...])

    for first, last in ((16, 36), (0, 16), (36, 48)):
        rows = slice(first * SLAB, last * SLAB)
        received(tgt_way, first, last)
        landed = tgt_in[first:last].reshape((last - first) * SLAB, ATT).astype(F32)
        upstream = dot((predicted[rows] - landed).astype(BF16), pw_ref[...])
        own = normed_h[rows]
        upstream_mean = jnp.mean(upstream, axis=-1, keepdims=True)
        cross_mean = jnp.mean(upstream * own, axis=-1, keepdims=True)
        grad_out[first:last] = to_slabs(
            inverses[rows] * (upstream - upstream_mean - own * cross_mean)
        )
        if first == 0:
            homeward(4, last)
            homeward_near()
        else:
            homeward(first, last)

    received(grad_way, 0, GRP)
    pg_ref[...] = dot(gather[...], grad_in[...].reshape(SLOTS, PRED)).astype(BF16)

    for copy in started:
        copy.wait_send()
    for h in range(HEADS):

        @pl.when(me != head_place(h))
        def _():
            pltpu.make_async_copy(head_out.at[h], head_in.at[0], head_send.at[h]).wait()

    @pl.when(is_head)
    def _():
        @pl.loop(1, SEQ)
        def _(k):
            to = lax.rem(me + k, SEQ)
            pltpu.make_async_copy(att_out.at[to], att_in.at[0], att_send.at[to]).wait()

    sent(hid_way, 0, GRP - 1)
    sent(tgt_way, 0, GRP - 1)
    sent(grad_way, 4, GRP)

    @pl.loop(1, 4)
    def _(k):
        j = lax.rem(yh + k, 4)
        pltpu.make_async_copy(grad_out.at[j], grad_in.at[j], grad_send.at[j]).wait()


def finish(nkv_in, tgt_in, pg_in, nkv_out, tgt_out, pg_out, sem):
    copies = [
        pltpu.make_async_copy(src, dst, sem.at[i])
        for i, (src, dst) in enumerate(((tgt_in, tgt_out), (nkv_in, nkv_out), (pg_in, pg_out)))
    ]
    for copy in copies:
        copy.start()
    for copy in copies:
        copy.wait()


def shards(
    tokens, target_kv, context_kv, query_weight, pred_hidden, pred_weight, target_mask, owners
):
    vmem = pl.BlockSpec(memory_space=pltpu.VMEM)
    dma = pltpu.SemaphoreType.DMA
    results = pl.pallas_call(
        kernel,
        out_shape=(
            jax.ShapeDtypeStruct((SHARD, D), BF16),
            jax.ShapeDtypeStruct((ATT, ROWS), BF16),
            jax.ShapeDtypeStruct((ROWS, PRED), BF16),
        ),
        in_specs=[pl.BlockSpec(memory_space=pl.ANY)] * 8,
        out_specs=(vmem,) * 3,
        scratch_shapes=[
            pltpu.VMEM((ROWS, D), BF16),
            pltpu.VMEM((SHARD, D), BF16),
            pltpu.VMEM((SHARD, D), BF16),
            pltpu.VMEM((ATT, D), BF16),
            pltpu.VMEM((ROWS, PRED), BF16),
            pltpu.VMEM((ATT, PRED), BF16),
            pltpu.VMEM((1, PAIRS), jnp.int32),
            pltpu.VMEM((1, PAIRS), jnp.int32),
            dma((8,)),
            pltpu.VMEM((SEQ, SHARD, D), BF16),
            pltpu.VMEM((SEQ, ROWS, SHARD), BF16),
            pltpu.VMEM((ROWS, D), F32),
            pltpu.VMEM((ROWS, ATT), F32),
            pltpu.VMEM((HEADS, ROWS + PAIRS, 2 * HEAD), BF16),
            pltpu.VMEM((SEQ, ROWS + PAIRS, 2 * HEAD), BF16),
            pltpu.VMEM((SEQ, ROWS, 2 * HEAD), BF16),
            pltpu.VMEM((SEQ, PAIRS, 2 * HEAD), BF16),
            pltpu.VMEM((HEADS, PAIRS, 2 * HEAD), BF16),
            pltpu.VMEM((SLOTS, ROWS), BF16),
            pltpu.VMEM((ROWS, SLOTS), BF16),
            pltpu.VMEM((GRP, SLAB, PRED), BF16),
            pltpu.VMEM((GRP, SLAB, PRED), BF16),
            pltpu.VMEM((GRP, SLAB, ATT), BF16),
            pltpu.VMEM((GRP, SLAB, ATT), BF16),
            pltpu.VMEM((GRP, SLAB, PRED), BF16),
            pltpu.VMEM((GRP, SLAB, PRED), BF16),
            pltpu.VMEM((SLOTS, ATT), F32),
            pltpu.VMEM((SLOTS, PRED), F32),
            pltpu.VMEM((SLOTS, 1), F32),
            dma((23,)),
            dma((23,)),
            dma((HEADS,)),
            dma((SEQ,)),
            dma((SEQ,)),
            dma((HEADS,)),
            dma((GRP,)),
            dma((GRP,)),
            dma((GRP,)),
            dma((GRP,)),
            dma((GRP,)),
            dma((GRP,)),
        ],
        compiler_params=pltpu.CompilerParams(
            collective_id=0, has_side_effects=True, vmem_limit_bytes=63 * 1024 * 1024
        ),
        cost_estimate=pl.CostEstimate(
            flops=2_000_000_000, bytes_accessed=5_000_000, transcendentals=3_000_000
        ),
        name="attend_and_route",
    )(
        tokens[0],
        target_kv,
        context_kv,
        query_weight,
        pred_hidden[0],
        pred_weight[0],
        target_mask,
        owners[0].reshape(1, PAIRS),
    )
    anywhere = pl.BlockSpec(memory_space=pl.ANY)
    new_kv, targets, pred_grad = pl.pallas_call(
        finish,
        out_shape=tuple(jax.ShapeDtypeStruct(r.shape, r.dtype) for r in results),
        in_specs=[anywhere] * 3,
        out_specs=(anywhere,) * 3,
        scratch_shapes=[dma((3,))],
        name="finish",
    )(*results)
    return new_kv, targets.T[None], pred_grad[None]


def solution(mesh):
    placed = (
        P("grp", "seq", None),
        P("seq", None),
        P("seq", None),
        P(),
        P("grp", "seq", None),
        P("grp", None, None),
        P("grp", "seq"),
        P("grp", "seq", None),
    )
    return jax.shard_map(
        shards,
        mesh=mesh,
        in_specs=placed,
        out_specs=(P("seq", None), P("grp", "seq", None), P("grp", "seq", None)),
        check_vma=False,
    )
```

```python
import math

import jax
import jax.numpy as jnp
from jax import lax
from jax.experimental import pallas as pl
from jax.experimental.pallas import tpu as pltpu
from jax.sharding import PartitionSpec as P

HEAD = 64
HEADS = 11
SEQ = 16
GRP = 48
ROWS = 128
PAIRS = 64
D = 1408
ATT = 704
PRED = 384
SHARD = 88
LO = 768
SLAB = 4
SLOTS = GRP * SLAB

keep_rate = 0.9
epsilon = 1e-05

F32 = jnp.float32
BF16 = jnp.bfloat16


def normalize(values):
    center = values - jnp.mean(values, axis=-1, keepdims=True)
    variance = jnp.mean(center * center, axis=-1, keepdims=True)
    inverse = lax.rsqrt(variance + epsilon)
    return center * inverse, inverse


def dot(a, b):
    return jnp.dot(a, b, preferred_element_type=F32)


def dot_t(a, b):
    return lax.dot_general(a, b, (((1,), (1,)), ((), ())), preferred_element_type=F32)


def iota(shape, axis):
    return lax.broadcasted_iota(jnp.int32, shape, axis)


def slot_rows(own_row, mask_row):
    shape = (PAIRS, PAIRS)
    down, across = iota(shape, 0), iota(shape, 1)
    same = down == across

    def turned(row):
        return jnp.broadcast_to(
            jnp.sum(jnp.where(same, row, 0.0), axis=1, keepdims=True), shape
        )

    own_across = jnp.broadcast_to(own_row, shape)
    live_across = jnp.broadcast_to(mask_row, shape)
    own_down, live_down = turned(own_across), turned(live_across)
    equal = own_down == own_across
    rank_row = jnp.sum(
        jnp.where(equal & (down < across), live_down, 0.0), axis=0, keepdims=True
    )
    rank_col = jnp.sum(
        jnp.where(equal & (across < down), live_across, 0.0), axis=1, keepdims=True
    )
    slot_row = jnp.where(mask_row > 0.5, own_across[:1] * 2.0 + rank_row, -1.0)
    slot_col = jnp.where(live_down[:, :1] > 0.5, own_down[:, :1] * 2.0 + rank_col, -1.0)
    shape = (PAIRS, ROWS)
    token_row = jnp.sum(
        jnp.where(
            iota(shape, 0) == lax.shift_right_logical(iota(shape, 1), 1),
            jnp.broadcast_to(slot_col, shape),
            0.0,
        ),
        axis=0,
        keepdims=True,
    )
    shape = (ROWS, PAIRS)
    token_col = jnp.sum(
        jnp.where(
            lax.shift_right_logical(iota(shape, 0), 1) == iota(shape, 1),
            jnp.broadcast_to(slot_row, shape),
            0.0,
        ),
        axis=1,
        keepdims=True,
    )
    return token_row, token_col


def dispatch_tables(own_row, mask_row):
    token_row, token_col = slot_rows(own_row, mask_row)
    shape = (SLOTS, ROWS)
    spread = jnp.where(
        (
            lax.shift_right_logical(iota(shape, 0), 1)
            == jnp.broadcast_to(token_row, shape).astype(jnp.int32)
        )
        & (lax.bitwise_and(iota(shape, 0), 1) == lax.bitwise_and(iota(shape, 1), 1)),
        1.0,
        0.0,
    ).astype(BF16)
    shape = (ROWS, SLOTS)
    gather = jnp.where(
        (
            lax.shift_right_logical(iota(shape, 1), 1)
            == jnp.broadcast_to(token_col, shape).astype(jnp.int32)
        )
        & (lax.bitwise_and(iota(shape, 0), 1) == lax.bitwise_and(iota(shape, 1), 1)),
        1.0,
        0.0,
    ).astype(BF16)
    return spread, gather


def kernel(
    tok_hbm,
    tkv_hbm,
    ckv_hbm,
    qw_hbm,
    hid_hbm,
    pw_hbm,
    mask_hbm,
    own_hbm,
    nkv_ref,
    tgt_ref,
    pg_ref,
    tok_ref,
    tkv_ref,
    ckv_ref,
    qw_ref,
    hid_ref,
    pw_ref,
    mask_ref,
    own_ref,
    load_sem,
    wbuf,
    chunks,
    acc,
    queries,
    head_out,
    head_in,
    values_one,
    att_out,
    att_in,
    spread,
    gather,
    hid_out,
    hid_in,
    tgt_out,
    tgt_in,
    grad_out,
    grad_in,
    predicted,
    normed_h,
    inverses,
    w_send,
    w_recv,
    head_send,
    head_recv,
    att_send,
    att_recv,
    hid_send,
    hid_recv,
    tgt_send,
    tgt_recv,
    grad_send,
    grad_recv,
):
    loads = [
        pltpu.make_async_copy(src, dst, load_sem.at[i])
        for i, (src, dst) in enumerate(
            (
                (tkv_hbm, tkv_ref),
                (ckv_hbm, ckv_ref),
                (tok_hbm, tok_ref),
                (qw_hbm, qw_ref),
                (mask_hbm, mask_ref),
                (own_hbm, own_ref),
                (hid_hbm, hid_ref),
                (pw_hbm, pw_ref),
            )
        )
    ]
    for load in loads:
        load.start()
    me = lax.axis_index("seq")
    mine = lax.axis_index("grp")
    core = lax.rem(me, 2)
    x = lax.rem(me // 2, 4)
    y = me // 8
    z = mine // 4
    yh = lax.rem(mine, 4)

    def place(xx, yy, cc):
        return (lax.rem(xx, 4) + yy * 4) * 2 + cc

    right, left, far = place(x + 1, y, core), place(x + 3, y, core), place(x + 2, y, core)
    across = place(x, 1 - y, core)
    right_p, left_p, far_p = (
        place(x + 1, 1 - y, core),
        place(x + 3, 1 - y, core),
        place(x + 2, 1 - y, core),
    )
    twin = place(x, y, 1 - core)
    up_grp = z * 4 + lax.rem(yh + y, 4)
    down_grp = z * 4 + lax.rem(yh + 3 * (1 - y), 4)
    other_grp = z * 4 + lax.rem(yh + 3 + 2 * y, 4)

    barrier = pltpu.get_barrier_semaphore()

    @pl.loop(1, SEQ)
    def _(k):
        pl.semaphore_signal(barrier, inc=1, device_id={"seq": lax.rem(me + k, SEQ), "grp": mine})

    @pl.loop(1, GRP)
    def _(k):
        pl.semaphore_signal(barrier, inc=1, device_id={"seq": me, "grp": lax.rem(mine + k, GRP)})

    pl.semaphore_signal(barrier, inc=1, device_id={"seq": across, "grp": other_grp})

    loads[0].wait()
    loads[1].wait()
    blended = (
        keep_rate * tkv_ref[...].astype(F32) + (1.0 - keep_rate) * ckv_ref[...].astype(F32)
    ).astype(BF16)
    nkv_ref[...] = blended
    wbuf[me] = blended
    pl.semaphore_wait(barrier, SEQ - 1 + GRP - 1 + 1)

    started = []

    def push(ref, slot, seq, grp):
        copy = pltpu.make_async_remote_copy(
            src_ref=ref,
            dst_ref=ref,
            send_sem=w_send.at[len(started)],
            recv_sem=w_recv.at[slot],
            device_id={"seq": seq, "grp": grp},
        )
        copy.start()
        started.append(copy)

    def arrive(ref, slot):
        pltpu.make_async_remote_copy(
            src_ref=ref,
            dst_ref=ref,
            send_sem=w_send.at[0],
            recv_sem=w_recv.at[slot],
            device_id={"seq": twin, "grp": mine},
        ).wait_recv()

    def lo(block):
        return wbuf.at[block, :, pl.ds(0, LO)]

    def hi(block):
        return wbuf.at[block, :, pl.ds(LO, D - LO)]

    push(lo(me), 0, right, mine)
    push(hi(me), 3, left, mine)
    push(lo(me), 4, across, up_grp)
    push(hi(me), 5, across, down_grp)
    push(hi(me), 1, right, mine)
    push(lo(me), 2, left, mine)
    push(wbuf.at[me], 14, twin, mine)

    loads[2].wait()
    normed = normalize(tok_ref[...].astype(F32))[0]
    for s in range(SEQ):
        chunks[s] = normed[:, s * SHARD : (s + 1) * SHARD].astype(BF16)
    normed_b = normed.astype(BF16)
    twin_of = 1 - 2 * core

    def term(block):
        return dot(chunks[block], wbuf[block])

    arrive(lo(left), 0)
    push(lo(left), 6, right, mine)
    push(lo(left), 8, across, up_grp)
    arrive(hi(right), 3)
    push(hi(right), 7, left, mine)
    push(hi(right), 11, across, down_grp)
    arrive(lo(across), 4)
    arrive(hi(across), 5)
    push(wbuf.at[across], 17, twin, mine)
    loads[3].wait()
    queries[...] = dot_t(normed_b, qw_ref[...])
    arrive(hi(left), 1)
    push(hi(left), 9, across, up_grp)
    push(wbuf.at[left], 15, twin, mine)
    arrive(lo(right), 2)
    push(lo(right), 10, across, down_grp)
    push(wbuf.at[right], 16, twin, mine)
    arrive(wbuf.at[twin], 14)
    acc[...] = term(me) + term(twin) + term(across)
    arrive(lo(left_p), 8)
    push(lo(left_p), 12, right, mine)
    arrive(hi(right_p), 11)
    push(hi(right_p), 13, left, mine)
    acc[...] += term(left) + term(right)
    arrive(lo(far), 6)
    arrive(hi(far), 7)
    push(wbuf.at[far], 18, twin, mine)
    arrive(wbuf.at[left + twin_of], 15)
    arrive(wbuf.at[right + twin_of], 16)
    arrive(wbuf.at[across + twin_of], 17)
    acc[...] += term(far) + term(left + twin_of) + term(right + twin_of) + term(across + twin_of)
    arrive(hi(left_p), 9)
    push(wbuf.at[left_p], 19, twin, mine)
    arrive(lo(right_p), 10)
    push(wbuf.at[right_p], 20, twin, mine)
    arrive(wbuf.at[far + twin_of], 18)
    acc[...] += term(left_p) + term(right_p) + term(far + twin_of)
    for load in loads[4:]:
        load.wait()
    spread[...], gather[...] = dispatch_tables(
        own_ref[...].astype(F32), mask_ref[...].astype(F32)
    )

    def to_slabs(rows):
        return rows.reshape(rows.shape[0] // SLAB, SLAB, rows.shape[1]).astype(BF16)

    hid_out[...] = to_slabs(dot(spread[...], hid_ref[...]))
    arrive(wbuf.at[left_p + twin_of], 19)
    arrive(wbuf.at[right_p + twin_of], 20)
    acc[...] += term(left_p + twin_of) + term(right_p + twin_of)
    arrive(lo(far_p), 12)
    push(lo(far_p), 21, twin, mine)
    arrive(hi(far_p), 13)
    push(hi(far_p), 22, twin, mine)
    acc[...] += term(far_p)
    arrive(lo(far_p + twin_of), 21)
    arrive(hi(far_p + twin_of), 22)
    acc[...] += term(far_p + twin_of)

    def head_place(h):
        return 2 * h if h < 8 else 1 + 4 * (h - 8)

    for h in range(HEADS):
        k_h = acc[:, h * HEAD : (h + 1) * HEAD]
        v_h = acc[:, ATT + h * HEAD : ATT + (h + 1) * HEAD]
        q_h = queries[:, h * HEAD : (h + 1) * HEAD]
        head_out[h, :ROWS] = jnp.concatenate([v_h, k_h], axis=1).astype(BF16)
        head_out[h, ROWS:] = jnp.concatenate([q_h[PAIRS:], q_h[:PAIRS]], axis=1).astype(BF16)
        to = head_place(h)

        @pl.when(me != to)
        def _():
            pltpu.make_async_remote_copy(
                src_ref=head_out.at[h],
                dst_ref=head_in.at[me],
                send_sem=head_send.at[h],
                recv_sem=head_recv.at[me],
                device_id={"seq": to, "grp": mine},
            ).start()

        @pl.when(me == to)
        def _():
            pltpu.make_async_copy(head_out.at[h], head_in.at[me], head_recv.at[me]).start()

    def outward(way, n):
        out, into, send, recv = way
        m = n // 4
        dz = GRP // 8 + (m + 1) // 2 * (1 - 2 * lax.rem(m, 2))
        to = lax.rem(z + dz, GRP // 4) * 4 + lax.rem(n, 4)
        slot = (GRP // 4 - dz) * 4 + yh
        pltpu.make_async_remote_copy(
            src_ref=out.at[to],
            dst_ref=into.at[slot],
            send_sem=send.at[n],
            recv_sem=recv.at[slot],
            device_id={"seq": me, "grp": to},
        ).start()

    def outward_near(way):
        out, into, send, recv = way

        @pl.loop(1, 4)
        def _(k):
            to = z * 4 + lax.rem(yh + k, 4)
            pltpu.make_async_remote_copy(
                src_ref=out.at[to],
                dst_ref=into.at[yh],
                send_sem=send.at[GRP - 5 + k],
                recv_sem=recv.at[yh],
                device_id={"seq": me, "grp": to},
            ).start()

        pltpu.make_async_copy(out.at[mine], into.at[yh], recv.at[yh]).start()

    def exchange(way):
        @pl.loop(0, GRP - 4)
        def _(n):
            outward(way, n)

        outward_near(way)

    def received(way, first, last):
        out, into, send, recv = way

        @pl.loop(first, last)
        def _(k):
            pltpu.make_async_copy(out.at[k], into.at[k], recv.at[k]).wait()

    def sent(way, first, last):
        out, into, send, recv = way

        @pl.loop(first, last)
        def _(k):
            pltpu.make_async_copy(out.at[k], into.at[k], send.at[k]).wait()

    def homeward(first, last):
        @pl.loop(first, last)
        def _(j):
            to = lax.rem(z + j // 4, GRP // 4) * 4 + lax.rem(j, 4)
            pltpu.make_async_remote_copy(
                src_ref=grad_out.at[j],
                dst_ref=grad_in.at[mine],
                send_sem=grad_send.at[j],
                recv_sem=grad_recv.at[mine],
                device_id={"seq": me, "grp": to},
            ).start()

    def homeward_near():
        @pl.loop(1, 4)
        def _(k):
            j = lax.rem(yh + k, 4)
            pltpu.make_async_remote_copy(
                src_ref=grad_out.at[j],
                dst_ref=grad_in.at[mine],
                send_sem=grad_send.at[j],
                recv_sem=grad_recv.at[mine],
                device_id={"seq": me, "grp": z * 4 + j},
            ).start()

        pltpu.make_async_copy(grad_out.at[yh], grad_in.at[mine], grad_recv.at[mine]).start()

    hid_way = (hid_out, hid_in, hid_send, hid_recv)
    tgt_way = (tgt_out, tgt_in, tgt_send, tgt_recv)
    grad_way = (grad_out, grad_in, grad_send, grad_recv)

    even = lax.rem(me, 2) == 0
    is_head = even | ((lax.rem(me, 4) == 1) & (me < 12))
    my_head = jnp.where(even, me // 2, 8 + me // 4)

    @pl.when(is_head)
    def _():
        @pl.loop(0, SEQ)
        def _(t):
            pltpu.make_async_copy(head_out.at[0], head_in.at[t], head_recv.at[t]).wait()

        lane = iota((ROWS, 2 * HEAD), 1)

        @pl.loop(0, SEQ)
        def _(t):
            block = head_in[t, :ROWS].astype(F32)
            values_one[t] = jnp.where(lane < HEAD, block, 1.0).astype(BF16)

        rate = math.log2(math.e) / math.sqrt(HEAD)

        @pl.loop(0, SEQ // 2)
        def _(i):
            zero = jnp.zeros((PAIRS, HEAD), BF16)
            parts = []
            for j in range(2):
                packed = head_in[2 * i + j, ROWS:]
                parts.append(jnp.concatenate([zero, packed[:, HEAD:]], axis=1))
                parts.append(jnp.concatenate([zero, packed[:, :HEAD]], axis=1))
            q = jnp.concatenate(parts, axis=0)
            for j in range(5):
                outward(hid_way, 5 * i + j)
            kv = head_in[:, :ROWS].reshape(SEQ * ROWS, 2 * HEAD)
            score = dot_t(q, kv)
            expo = jnp.exp2(score * rate).astype(BF16)
            added = dot(expo, values_one[...].reshape(SEQ * ROWS, 2 * HEAD))
            attended = added[:, :HEAD] / added[:, HEAD:]
            for j in range(2):
                rows = attended[j * ROWS : (j + 1) * ROWS]
                to = 2 * i + j
                att_out[to] = jnp.concatenate([rows[:PAIRS], rows[PAIRS:]], axis=1).astype(BF16)

                @pl.when(me != to)
                def _():
                    pltpu.make_async_remote_copy(
                        src_ref=att_out.at[to],
                        dst_ref=att_in.at[my_head],
                        send_sem=att_send.at[to],
                        recv_sem=att_recv.at[my_head],
                        device_id={"seq": to, "grp": mine},
                    ).start()

                @pl.when(me == to)
                def _():
                    pltpu.make_async_copy(
                        att_out.at[to], att_in.at[my_head], att_recv.at[my_head]
                    ).start()

        @pl.loop(5 * SEQ // 2, GRP - 4)
        def _(n):
            outward(hid_way, n)

        outward_near(hid_way)

    @pl.when(jnp.logical_not(is_head))
    def _():
        exchange(hid_way)

    @pl.loop(0, HEADS)
    def _(h):
        pltpu.make_async_copy(att_out.at[0], att_in.at[h], att_recv.at[h]).wait()

    top = jnp.concatenate([att_in[h][:, :HEAD].astype(F32) for h in range(HEADS)], axis=1)
    low = jnp.concatenate([att_in[h][:, HEAD:].astype(F32) for h in range(HEADS)], axis=1)
    attended = jnp.concatenate([top, low], axis=0)
    targets = normalize(attended)[0]
    tgt_out[...] = to_slabs(dot(spread[...], targets.astype(BF16)))
    exchange(tgt_way)
    tgt_ref[...] = targets.T.astype(BF16)

    received(hid_way, 0, GRP)
    owned, inverse = normalize(hid_in[...].reshape(SLOTS, PRED).astype(F32))
    normed_h[...] = owned
    inverses[...] = inverse
    predicted[...] = dot_t(owned.astype(BF16), pw_ref[...])

    for first, last in ((16, 36), (0, 16), (36, 48)):
        rows = slice(first * SLAB, last * SLAB)
        received(tgt_way, first, last)
        landed = tgt_in[first:last].reshape((last - first) * SLAB, ATT).astype(F32)
        upstream = dot((predicted[rows] - landed).astype(BF16), pw_ref[...])
        own = normed_h[rows]
        upstream_mean = jnp.mean(upstream, axis=-1, keepdims=True)
        cross_mean = jnp.mean(upstream * own, axis=-1, keepdims=True)
        grad_out[first:last] = to_slabs(
            inverses[rows] * (upstream - upstream_mean - own * cross_mean)
        )
        if first == 0:
            homeward(4, last)
            homeward_near()
        else:
            homeward(first, last)

    received(grad_way, 0, GRP)
    pg_ref[...] = dot(gather[...], grad_in[...].reshape(SLOTS, PRED)).astype(BF16)

    for copy in started:
        copy.wait_send()
    for h in range(HEADS):

        @pl.when(me != head_place(h))
        def _():
            pltpu.make_async_copy(head_out.at[h], head_in.at[0], head_send.at[h]).wait()

    @pl.when(is_head)
    def _():
        @pl.loop(1, SEQ)
        def _(k):
            to = lax.rem(me + k, SEQ)
            pltpu.make_async_copy(att_out.at[to], att_in.at[0], att_send.at[to]).wait()

    sent(hid_way, 0, GRP - 1)
    sent(tgt_way, 0, GRP - 1)
    sent(grad_way, 4, GRP)

    @pl.loop(1, 4)
    def _(k):
        j = lax.rem(yh + k, 4)
        pltpu.make_async_copy(grad_out.at[j], grad_in.at[j], grad_send.at[j]).wait()


def finish(nkv_in, tgt_in, pg_in, nkv_out, tgt_out, pg_out, sem):
    copies = [
        pltpu.make_async_copy(src, dst, sem.at[i])
        for i, (src, dst) in enumerate(((tgt_in, tgt_out), (nkv_in, nkv_out), (pg_in, pg_out)))
    ]
    for copy in copies:
        copy.start()
    for copy in copies:
        copy.wait()


def shards(
    tokens, target_kv, context_kv, query_weight, pred_hidden, pred_weight, target_mask, owners
):
    vmem = pl.BlockSpec(memory_space=pltpu.VMEM)
    dma = pltpu.SemaphoreType.DMA
    results = pl.pallas_call(
        kernel,
        out_shape=(
            pltpu.VMEM((SHARD, D), BF16),
            pltpu.VMEM((ATT, ROWS), BF16),
            pltpu.VMEM((ROWS, PRED), BF16),
        ),
        in_specs=[pl.BlockSpec(memory_space=pl.ANY)] * 8,
        out_specs=(vmem,) * 3,
        scratch_shapes=[
            pltpu.VMEM((ROWS, D), BF16),
            pltpu.VMEM((SHARD, D), BF16),
            pltpu.VMEM((SHARD, D), BF16),
            pltpu.VMEM((ATT, D), BF16),
            pltpu.VMEM((ROWS, PRED), BF16),
            pltpu.VMEM((ATT, PRED), BF16),
            pltpu.VMEM((1, PAIRS), jnp.int32),
            pltpu.VMEM((1, PAIRS), jnp.int32),
            dma((8,)),
            pltpu.VMEM((SEQ, SHARD, D), BF16),
            pltpu.VMEM((SEQ, ROWS, SHARD), BF16),
            pltpu.VMEM((ROWS, D), F32),
            pltpu.VMEM((ROWS, ATT), F32),
            pltpu.VMEM((HEADS, ROWS + PAIRS, 2 * HEAD), BF16),
            pltpu.VMEM((SEQ, ROWS + PAIRS, 2 * HEAD), BF16),
            pltpu.VMEM((SEQ, ROWS, 2 * HEAD), BF16),
            pltpu.VMEM((SEQ, PAIRS, 2 * HEAD), BF16),
            pltpu.VMEM((HEADS, PAIRS, 2 * HEAD), BF16),
            pltpu.VMEM((SLOTS, ROWS), BF16),
            pltpu.VMEM((ROWS, SLOTS), BF16),
            pltpu.VMEM((GRP, SLAB, PRED), BF16),
            pltpu.VMEM((GRP, SLAB, PRED), BF16),
            pltpu.VMEM((GRP, SLAB, ATT), BF16),
            pltpu.VMEM((GRP, SLAB, ATT), BF16),
            pltpu.VMEM((GRP, SLAB, PRED), BF16),
            pltpu.VMEM((GRP, SLAB, PRED), BF16),
            pltpu.VMEM((SLOTS, ATT), F32),
            pltpu.VMEM((SLOTS, PRED), F32),
            pltpu.VMEM((SLOTS, 1), F32),
            dma((23,)),
            dma((23,)),
            dma((HEADS,)),
            dma((SEQ,)),
            dma((SEQ,)),
            dma((HEADS,)),
            dma((GRP,)),
            dma((GRP,)),
            dma((GRP,)),
            dma((GRP,)),
            dma((GRP,)),
            dma((GRP,)),
        ],
        compiler_params=pltpu.CompilerParams(
            collective_id=0, has_side_effects=True, vmem_limit_bytes=56 * 1024 * 1024
        ),
        cost_estimate=pl.CostEstimate(
            flops=2_000_000_000, bytes_accessed=5_000_000, transcendentals=3_000_000
        ),
        name="attend_and_route",
    )(
        *(
            pltpu.with_memory_space_constraint(argument, pltpu.HBM)
            for argument in (
                tokens[0],
                target_kv,
                context_kv,
                query_weight,
                pred_hidden[0],
                pred_weight[0],
                target_mask,
                owners[0].reshape(1, PAIRS),
            )
        )
    )
    anywhere = pl.BlockSpec(memory_space=pl.ANY)
    new_kv, targets, pred_grad = pl.pallas_call(
        finish,
        out_shape=tuple(jax.ShapeDtypeStruct(r.shape, r.dtype) for r in results),
        in_specs=[anywhere] * 3,
        out_specs=(anywhere,) * 3,
        scratch_shapes=[dma((3,))],
        name="finish",
    )(*(pltpu.with_memory_space_constraint(r, pltpu.VMEM) for r in results))
    return new_kv, targets.T[None], pred_grad[None]


def solution(mesh):
    placed = (
        P("grp", "seq", None),
        P("seq", None),
        P("seq", None),
        P(),
        P("grp", "seq", None),
        P("grp", None, None),
        P("grp", "seq"),
        P("grp", "seq", None),
    )
    return jax.shard_map(
        shards,
        mesh=mesh,
        in_specs=placed,
        out_specs=(P("seq", None), P("grp", "seq", None), P("grp", "seq", None)),
        check_vma=False,
    )
```

```python
import math

import jax
import jax.numpy as jnp
from jax import lax
from jax.experimental import pallas as pl
from jax.experimental.pallas import tpu as pltpu
from jax.sharding import PartitionSpec as P

HEAD = 64
HEADS = 11
SEQ = 16
GRP = 48
ROWS = 128
PAIRS = 64
D = 1408
ATT = 704
PRED = 384
SHARD = 88
LO = 768
SLAB = 4
BURST = 8
SLOTS = GRP * SLAB

keep_rate = 0.9
epsilon = 1e-05

F32 = jnp.float32
BF16 = jnp.bfloat16


def normalize(values):
    center = values - jnp.mean(values, axis=-1, keepdims=True)
    variance = jnp.mean(center * center, axis=-1, keepdims=True)
    inverse = lax.rsqrt(variance + epsilon)
    return center * inverse, inverse


def dot(a, b):
    return jnp.dot(a, b, preferred_element_type=F32)


def dot_t(a, b):
    return lax.dot_general(a, b, (((1,), (1,)), ((), ())), preferred_element_type=F32)


def iota(shape, axis):
    return lax.broadcasted_iota(jnp.int32, shape, axis)


def slot_rows(own_row, mask_row):
    shape = (PAIRS, PAIRS)
    down, across = iota(shape, 0), iota(shape, 1)
    same = down == across

    def turned(row):
        return jnp.broadcast_to(
            jnp.sum(jnp.where(same, row, 0.0), axis=1, keepdims=True), shape
        )

    own_across = jnp.broadcast_to(own_row, shape)
    live_across = jnp.broadcast_to(mask_row, shape)
    own_down, live_down = turned(own_across), turned(live_across)
    equal = own_down == own_across
    rank_row = jnp.sum(
        jnp.where(equal & (down < across), live_down, 0.0), axis=0, keepdims=True
    )
    rank_col = jnp.sum(
        jnp.where(equal & (across < down), live_across, 0.0), axis=1, keepdims=True
    )
    slot_row = jnp.where(mask_row > 0.5, own_across[:1] * 2.0 + rank_row, -1.0)
    slot_col = jnp.where(live_down[:, :1] > 0.5, own_down[:, :1] * 2.0 + rank_col, -1.0)
    shape = (PAIRS, ROWS)
    token_row = jnp.sum(
        jnp.where(
            iota(shape, 0) == lax.shift_right_logical(iota(shape, 1), 1),
            jnp.broadcast_to(slot_col, shape),
            0.0,
        ),
        axis=0,
        keepdims=True,
    )
    shape = (ROWS, PAIRS)
    token_col = jnp.sum(
        jnp.where(
            lax.shift_right_logical(iota(shape, 0), 1) == iota(shape, 1),
            jnp.broadcast_to(slot_row, shape),
            0.0,
        ),
        axis=1,
        keepdims=True,
    )
    return token_row, token_col


def dispatch_tables(own_row, mask_row):
    token_row, token_col = slot_rows(own_row, mask_row)
    shape = (SLOTS, ROWS)
    spread = jnp.where(
        (
            lax.shift_right_logical(iota(shape, 0), 1)
            == jnp.broadcast_to(token_row, shape).astype(jnp.int32)
        )
        & (lax.bitwise_and(iota(shape, 0), 1) == lax.bitwise_and(iota(shape, 1), 1)),
        1.0,
        0.0,
    ).astype(BF16)
    shape = (ROWS, SLOTS)
    gather = jnp.where(
        (
            lax.shift_right_logical(iota(shape, 1), 1)
            == jnp.broadcast_to(token_col, shape).astype(jnp.int32)
        )
        & (lax.bitwise_and(iota(shape, 0), 1) == lax.bitwise_and(iota(shape, 1), 1)),
        1.0,
        0.0,
    ).astype(BF16)
    return spread, gather


def kernel(
    tok_hbm,
    tkv_hbm,
    ckv_hbm,
    qw_hbm,
    hid_hbm,
    pw_hbm,
    mask_hbm,
    own_hbm,
    nkv_ref,
    tgt_ref,
    pg_ref,
    tok_ref,
    tkv_ref,
    ckv_ref,
    qw_ref,
    hid_ref,
    pw_ref,
    mask_ref,
    own_ref,
    load_sem,
    wbuf,
    chunks,
    acc,
    queries,
    head_out,
    head_in,
    values_one,
    att_out,
    att_in,
    spread,
    gather,
    hid_out,
    hid_in,
    tgt_out,
    tgt_in,
    grad_out,
    grad_in,
    predicted,
    normed_h,
    inverses,
    w_send,
    w_recv,
    head_send,
    head_recv,
    att_send,
    att_recv,
    hid_send,
    hid_recv,
    tgt_send,
    tgt_recv,
    grad_send,
    grad_recv,
):
    loads = [
        pltpu.make_async_copy(src, dst, load_sem.at[i])
        for i, (src, dst) in enumerate(
            (
                (tkv_hbm, tkv_ref),
                (ckv_hbm, ckv_ref),
                (tok_hbm, tok_ref),
                (qw_hbm, qw_ref),
                (mask_hbm, mask_ref),
                (own_hbm, own_ref),
                (hid_hbm, hid_ref),
                (pw_hbm, pw_ref),
            )
        )
    ]
    for load in loads:
        load.start()
    me = lax.axis_index("seq")
    mine = lax.axis_index("grp")
    core = lax.rem(me, 2)
    x = lax.rem(me // 2, 4)
    y = me // 8
    z = mine // 4
    yh = lax.rem(mine, 4)

    def place(xx, yy, cc):
        return (lax.rem(xx, 4) + yy * 4) * 2 + cc

    right, left, far = place(x + 1, y, core), place(x + 3, y, core), place(x + 2, y, core)
    across = place(x, 1 - y, core)
    right_p, left_p, far_p = (
        place(x + 1, 1 - y, core),
        place(x + 3, 1 - y, core),
        place(x + 2, 1 - y, core),
    )
    twin = place(x, y, 1 - core)
    up_grp = z * 4 + lax.rem(yh + y, 4)
    down_grp = z * 4 + lax.rem(yh + 3 * (1 - y), 4)
    other_grp = z * 4 + lax.rem(yh + 3 + 2 * y, 4)

    def lane_of(to_yh):
        return jnp.where(lax.rem(to_yh - yh + 4, 4) == 2, across, me)

    barrier = pltpu.get_barrier_semaphore()

    @pl.loop(1, SEQ)
    def _(k):
        pl.semaphore_signal(barrier, inc=1, device_id={"seq": lax.rem(me + k, SEQ), "grp": mine})

    @pl.loop(1, GRP)
    def _(k):
        to = lax.rem(mine + k, GRP)
        pl.semaphore_signal(
            barrier, inc=1, device_id={"seq": lane_of(lax.rem(to, 4)), "grp": to}
        )

    pl.semaphore_signal(barrier, inc=1, device_id={"seq": across, "grp": other_grp})

    loads[0].wait()
    loads[1].wait()
    blended = (
        keep_rate * tkv_ref[...].astype(F32) + (1.0 - keep_rate) * ckv_ref[...].astype(F32)
    ).astype(BF16)
    nkv_ref[...] = blended
    wbuf[me] = blended
    pl.semaphore_wait(barrier, SEQ - 1 + GRP - 1 + 1)

    started = []

    def push(ref, slot, seq, grp):
        copy = pltpu.make_async_remote_copy(
            src_ref=ref,
            dst_ref=ref,
            send_sem=w_send.at[len(started)],
            recv_sem=w_recv.at[slot],
            device_id={"seq": seq, "grp": grp},
        )
        copy.start()
        started.append(copy)

    def arrive(ref, slot):
        pltpu.make_async_remote_copy(
            src_ref=ref,
            dst_ref=ref,
            send_sem=w_send.at[0],
            recv_sem=w_recv.at[slot],
            device_id={"seq": twin, "grp": mine},
        ).wait_recv()

    def lo(block):
        return wbuf.at[block, :, pl.ds(0, LO)]

    def hi(block):
        return wbuf.at[block, :, pl.ds(LO, D - LO)]

    push(lo(me), 0, right, mine)
    push(hi(me), 3, left, mine)
    push(lo(me), 4, across, up_grp)
    push(hi(me), 5, across, down_grp)
    push(hi(me), 1, right, mine)
    push(lo(me), 2, left, mine)
    push(wbuf.at[me], 14, twin, mine)

    loads[2].wait()
    normed = normalize(tok_ref[...].astype(F32))[0]
    for s in range(SEQ):
        chunks[s] = normed[:, s * SHARD : (s + 1) * SHARD].astype(BF16)
    normed_b = normed.astype(BF16)
    twin_of = 1 - 2 * core

    def term(block):
        return dot(chunks[block], wbuf[block])

    arrive(lo(left), 0)
    push(lo(left), 6, right, mine)
    push(lo(left), 8, across, up_grp)
    arrive(hi(right), 3)
    push(hi(right), 7, left, mine)
    push(hi(right), 11, across, down_grp)
    arrive(lo(across), 4)
    arrive(hi(across), 5)
    push(wbuf.at[across], 17, twin, mine)
    loads[3].wait()
    queries[...] = dot_t(normed_b, qw_ref[...])
    arrive(hi(left), 1)
    push(hi(left), 9, across, up_grp)
    push(wbuf.at[left], 15, twin, mine)
    arrive(lo(right), 2)
    push(lo(right), 10, across, down_grp)
    push(wbuf.at[right], 16, twin, mine)
    arrive(wbuf.at[twin], 14)
    acc[...] = term(me) + term(twin) + term(across)
    arrive(lo(left_p), 8)
    push(lo(left_p), 12, right, mine)
    arrive(hi(right_p), 11)
    push(hi(right_p), 13, left, mine)
    acc[...] += term(left) + term(right)
    arrive(lo(far), 6)
    arrive(hi(far), 7)
    push(wbuf.at[far], 18, twin, mine)
    arrive(wbuf.at[left + twin_of], 15)
    arrive(wbuf.at[right + twin_of], 16)
    arrive(wbuf.at[across + twin_of], 17)
    acc[...] += term(far) + term(left + twin_of) + term(right + twin_of) + term(across + twin_of)
    arrive(hi(left_p), 9)
    push(wbuf.at[left_p], 19, twin, mine)
    arrive(lo(right_p), 10)
    push(wbuf.at[right_p], 20, twin, mine)
    arrive(wbuf.at[far + twin_of], 18)
    acc[...] += term(left_p) + term(right_p) + term(far + twin_of)
    for load in loads[4:]:
        load.wait()
    spread[...], gather[...] = dispatch_tables(
        own_ref[...].astype(F32), mask_ref[...].astype(F32)
    )

    def to_slabs(rows):
        return rows.reshape(rows.shape[0] // SLAB, SLAB, rows.shape[1]).astype(BF16)

    hid_out[...] = to_slabs(dot(spread[...], hid_ref[...]))
    arrive(wbuf.at[left_p + twin_of], 19)
    arrive(wbuf.at[right_p + twin_of], 20)
    acc[...] += term(left_p + twin_of) + term(right_p + twin_of)
    arrive(lo(far_p), 12)
    push(lo(far_p), 21, twin, mine)
    arrive(hi(far_p), 13)
    push(hi(far_p), 22, twin, mine)
    acc[...] += term(far_p)
    arrive(lo(far_p + twin_of), 21)
    arrive(hi(far_p + twin_of), 22)
    acc[...] += term(far_p + twin_of)

    def head_place(h):
        return jnp.where(h < 8, 2 * h, 4 * h - 31)

    for h in range(HEADS):
        k_h = acc[:, h * HEAD : (h + 1) * HEAD]
        v_h = acc[:, ATT + h * HEAD : ATT + (h + 1) * HEAD]
        q_h = queries[:, h * HEAD : (h + 1) * HEAD]
        head_out[h, :ROWS] = jnp.concatenate([v_h, k_h], axis=1).astype(BF16)
        head_out[h, ROWS:] = jnp.concatenate([q_h[PAIRS:], q_h[:PAIRS]], axis=1).astype(BF16)

    @pl.loop(0, HEADS)
    def _(k):
        h = lax.rem(me + k, HEADS)
        to = head_place(h)

        @pl.when(me != to)
        def _():
            pltpu.make_async_remote_copy(
                src_ref=head_out.at[h],
                dst_ref=head_in.at[me],
                send_sem=head_send.at[h],
                recv_sem=head_recv.at[me],
                device_id={"seq": to, "grp": mine},
            ).start()

        @pl.when(me == to)
        def _():
            pltpu.make_async_copy(head_out.at[h], head_in.at[me], head_recv.at[me]).start()

    def outward(way):
        out, into, send, recv = way

        @pl.loop(0, GRP // 4 - 1)
        def _(m):
            dz = GRP // 8 + (m + 1) // 2 * (1 - 2 * lax.rem(m, 2))
            base = lax.rem(z + dz, GRP // 4) * 4
            slot = (GRP // 4 - dz) * 4 + yh
            for c in range(4):
                pltpu.make_async_remote_copy(
                    src_ref=out.at[base + c],
                    dst_ref=into.at[slot],
                    send_sem=send.at[m * 4 + c],
                    recv_sem=recv.at[slot],
                    device_id={"seq": lane_of(c), "grp": base + c},
                ).start()

    def outward_near(way):
        out, into, send, recv = way

        @pl.loop(1, 4)
        def _(k):
            to = z * 4 + lax.rem(yh + k, 4)
            pltpu.make_async_remote_copy(
                src_ref=out.at[to],
                dst_ref=into.at[yh],
                send_sem=send.at[GRP - 5 + k],
                recv_sem=recv.at[yh],
                device_id={"seq": jnp.where(k == 2, across, me), "grp": to},
            ).start()

        pltpu.make_async_copy(out.at[mine], into.at[yh], recv.at[yh]).start()

    def exchange(way):
        outward(way)
        outward_near(way)

    def received(way, first, last):
        out, into, send, recv = way

        @pl.loop(first, last)
        def _(k):
            pltpu.make_async_copy(out.at[k], into.at[k], recv.at[k]).wait()

    def sent(way, first, last):
        out, into, send, recv = way

        @pl.loop(first, last)
        def _(k):
            pltpu.make_async_copy(out.at[k], into.at[k], send.at[k]).wait()

    def homeward(first, last):
        @pl.loop(first // 4, last // 4)
        def _(dz):
            base = lax.rem(z + dz, GRP // 4) * 4
            for c in range(4):
                pltpu.make_async_remote_copy(
                    src_ref=grad_out.at[dz * 4 + c],
                    dst_ref=grad_in.at[mine],
                    send_sem=grad_send.at[dz * 4 + c],
                    recv_sem=grad_recv.at[mine],
                    device_id={"seq": lane_of(c), "grp": base + c},
                ).start()

    def homeward_near():
        @pl.loop(1, 4)
        def _(k):
            j = lax.rem(yh + k, 4)
            pltpu.make_async_remote_copy(
                src_ref=grad_out.at[j],
                dst_ref=grad_in.at[mine],
                send_sem=grad_send.at[j],
                recv_sem=grad_recv.at[mine],
                device_id={"seq": jnp.where(k == 2, across, me), "grp": z * 4 + j},
            ).start()

        pltpu.make_async_copy(grad_out.at[yh], grad_in.at[mine], grad_recv.at[mine]).start()

    hid_way = (hid_out, hid_in, hid_send, hid_recv)
    tgt_way = (tgt_out, tgt_in, tgt_send, tgt_recv)
    grad_way = (grad_out, grad_in, grad_send, grad_recv)

    exchange(hid_way)

    even = lax.rem(me, 2) == 0
    is_head = even | ((lax.rem(me, 4) == 1) & (me < 12))
    my_head = jnp.where(even, me // 2, 8 + me // 4)

    @pl.when(is_head)
    def _():
        lane = iota((ROWS, 2 * HEAD), 1)

        @pl.loop(0, SEQ)
        def _(t):
            pltpu.make_async_copy(head_out.at[0], head_in.at[t], head_recv.at[t]).wait()
            block = head_in[t, :ROWS].astype(F32)
            values_one[t] = jnp.where(lane < HEAD, block, 1.0).astype(BF16)

        rate = math.log2(math.e) / math.sqrt(HEAD)

        @pl.loop(0, SEQ // BURST)
        def _(i):
            zero = jnp.zeros((PAIRS, HEAD), BF16)
            parts = []
            for j in range(BURST):
                packed = head_in[BURST * i + j, ROWS:]
                parts.append(jnp.concatenate([zero, packed[:, HEAD:]], axis=1))
                parts.append(jnp.concatenate([zero, packed[:, :HEAD]], axis=1))
            q = jnp.concatenate(parts, axis=0)
            kv = head_in[:, :ROWS].reshape(SEQ * ROWS, 2 * HEAD)
            score = dot_t(q, kv)
            expo = jnp.exp2(score * rate).astype(BF16)
            added = dot(expo, values_one[...].reshape(SEQ * ROWS, 2 * HEAD))
            attended = added[:, :HEAD] / added[:, HEAD:]
            for j in range(BURST):
                rows = attended[j * ROWS : (j + 1) * ROWS]
                att_out[BURST * i + j] = jnp.concatenate(
                    [rows[:PAIRS], rows[PAIRS:]], axis=1
                ).astype(BF16)

            @pl.loop(0, BURST)
            def _(k):
                to = BURST * i + lax.rem(me + k, BURST)

                @pl.when(me != to)
                def _():
                    pltpu.make_async_remote_copy(
                        src_ref=att_out.at[to],
                        dst_ref=att_in.at[my_head],
                        send_sem=att_send.at[to],
                        recv_sem=att_recv.at[my_head],
                        device_id={"seq": to, "grp": mine},
                    ).start()

                @pl.when(me == to)
                def _():
                    pltpu.make_async_copy(
                        att_out.at[to], att_in.at[my_head], att_recv.at[my_head]
                    ).start()

    @pl.loop(0, HEADS)
    def _(h):
        pltpu.make_async_copy(att_out.at[0], att_in.at[h], att_recv.at[h]).wait()

    top = jnp.concatenate([att_in[h][:, :HEAD].astype(F32) for h in range(HEADS)], axis=1)
    low = jnp.concatenate([att_in[h][:, HEAD:].astype(F32) for h in range(HEADS)], axis=1)
    attended = jnp.concatenate([top, low], axis=0)
    targets = normalize(attended)[0]
    tgt_out[...] = to_slabs(dot(spread[...], targets.astype(BF16)))
    exchange(tgt_way)
    tgt_ref[...] = targets.T.astype(BF16)

    received(hid_way, 0, GRP)
    owned, inverse = normalize(hid_in[...].reshape(SLOTS, PRED).astype(F32))
    normed_h[...] = owned
    inverses[...] = inverse
    predicted[...] = dot_t(owned.astype(BF16), pw_ref[...])

    for first, last in ((16, 36), (0, 16), (36, 48)):
        rows = slice(first * SLAB, last * SLAB)
        received(tgt_way, first, last)
        landed = tgt_in[first:last].reshape((last - first) * SLAB, ATT).astype(F32)
        upstream = dot((predicted[rows] - landed).astype(BF16), pw_ref[...])
        own = normed_h[rows]
        upstream_mean = jnp.mean(upstream, axis=-1, keepdims=True)
        cross_mean = jnp.mean(upstream * own, axis=-1, keepdims=True)
        grad_out[first:last] = to_slabs(
            inverses[rows] * (upstream - upstream_mean - own * cross_mean)
        )
        if first == 0:
            homeward(4, last)
            homeward_near()
        else:
            homeward(first, last)

    received(grad_way, 0, GRP)
    pg_ref[...] = dot(gather[...], grad_in[...].reshape(SLOTS, PRED)).astype(BF16)

    for copy in started:
        copy.wait_send()
    for h in range(HEADS):

        @pl.when(me != head_place(h))
        def _():
            pltpu.make_async_copy(head_out.at[h], head_in.at[0], head_send.at[h]).wait()

    @pl.when(is_head)
    def _():
        @pl.loop(1, SEQ)
        def _(k):
            to = lax.rem(me + k, SEQ)
            pltpu.make_async_copy(att_out.at[to], att_in.at[0], att_send.at[to]).wait()

    sent(hid_way, 0, GRP - 1)
    sent(tgt_way, 0, GRP - 1)
    sent(grad_way, 4, GRP)

    @pl.loop(1, 4)
    def _(k):
        j = lax.rem(yh + k, 4)
        pltpu.make_async_copy(grad_out.at[j], grad_in.at[j], grad_send.at[j]).wait()


def finish(nkv_in, tgt_in, pg_in, nkv_out, tgt_out, pg_out, sem):
    copies = [
        pltpu.make_async_copy(src, dst, sem.at[i])
        for i, (src, dst) in enumerate(((tgt_in, tgt_out), (nkv_in, nkv_out), (pg_in, pg_out)))
    ]
    for copy in copies:
        copy.start()
    for copy in copies:
        copy.wait()


def shards(
    tokens, target_kv, context_kv, query_weight, pred_hidden, pred_weight, target_mask, owners
):
    vmem = pl.BlockSpec(memory_space=pltpu.VMEM)
    dma = pltpu.SemaphoreType.DMA
    results = pl.pallas_call(
        kernel,
        out_shape=(
            pltpu.VMEM((SHARD, D), BF16),
            pltpu.VMEM((ATT, ROWS), BF16),
            pltpu.VMEM((ROWS, PRED), BF16),
        ),
        in_specs=[pl.BlockSpec(memory_space=pl.ANY)] * 8,
        out_specs=(vmem,) * 3,
        scratch_shapes=[
            pltpu.VMEM((ROWS, D), BF16),
            pltpu.VMEM((SHARD, D), BF16),
            pltpu.VMEM((SHARD, D), BF16),
            pltpu.VMEM((ATT, D), BF16),
            pltpu.VMEM((ROWS, PRED), BF16),
            pltpu.VMEM((ATT, PRED), BF16),
            pltpu.VMEM((1, PAIRS), jnp.int32),
            pltpu.VMEM((1, PAIRS), jnp.int32),
            dma((8,)),
            pltpu.VMEM((SEQ, SHARD, D), BF16),
            pltpu.VMEM((SEQ, ROWS, SHARD), BF16),
            pltpu.VMEM((ROWS, D), F32),
            pltpu.VMEM((ROWS, ATT), F32),
            pltpu.VMEM((HEADS, ROWS + PAIRS, 2 * HEAD), BF16),
            pltpu.VMEM((SEQ, ROWS + PAIRS, 2 * HEAD), BF16),
            pltpu.VMEM((SEQ, ROWS, 2 * HEAD), BF16),
            pltpu.VMEM((SEQ, PAIRS, 2 * HEAD), BF16),
            pltpu.VMEM((HEADS, PAIRS, 2 * HEAD), BF16),
            pltpu.VMEM((SLOTS, ROWS), BF16),
            pltpu.VMEM((ROWS, SLOTS), BF16),
            pltpu.VMEM((GRP, SLAB, PRED), BF16),
            pltpu.VMEM((GRP, SLAB, PRED), BF16),
            pltpu.VMEM((GRP, SLAB, ATT), BF16),
            pltpu.VMEM((GRP, SLAB, ATT), BF16),
            pltpu.VMEM((GRP, SLAB, PRED), BF16),
            pltpu.VMEM((GRP, SLAB, PRED), BF16),
            pltpu.VMEM((SLOTS, ATT), F32),
            pltpu.VMEM((SLOTS, PRED), F32),
            pltpu.VMEM((SLOTS, 1), F32),
            dma((23,)),
            dma((23,)),
            dma((HEADS,)),
            dma((SEQ,)),
            dma((SEQ,)),
            dma((HEADS,)),
            dma((GRP,)),
            dma((GRP,)),
            dma((GRP,)),
            dma((GRP,)),
            dma((GRP,)),
            dma((GRP,)),
        ],
        compiler_params=pltpu.CompilerParams(
            collective_id=0, has_side_effects=True, vmem_limit_bytes=56 * 1024 * 1024
        ),
        cost_estimate=pl.CostEstimate(
            flops=2_000_000_000, bytes_accessed=5_000_000, transcendentals=3_000_000
        ),
        name="attend_and_route",
    )(
        *(
            pltpu.with_memory_space_constraint(argument, pltpu.HBM)
            for argument in (
                tokens[0],
                target_kv,
                context_kv,
                query_weight,
                pred_hidden[0],
                pred_weight[0],
                target_mask,
                owners[0].reshape(1, PAIRS),
            )
        )
    )
    anywhere = pl.BlockSpec(memory_space=pl.ANY)
    new_kv, targets, pred_grad = pl.pallas_call(
        finish,
        out_shape=tuple(jax.ShapeDtypeStruct(r.shape, r.dtype) for r in results),
        in_specs=[anywhere] * 3,
        out_specs=(anywhere,) * 3,
        scratch_shapes=[dma((3,))],
        name="finish",
    )(*(pltpu.with_memory_space_constraint(r, pltpu.VMEM) for r in results))
    return new_kv, targets.T[None], pred_grad[None]


def solution(mesh):
    placed = (
        P("grp", "seq", None),
        P("seq", None),
        P("seq", None),
        P(),
        P("grp", "seq", None),
        P("grp", None, None),
        P("grp", "seq"),
        P("grp", "seq", None),
    )
    return jax.shard_map(
        shards,
        mesh=mesh,
        in_specs=placed,
        out_specs=(P("seq", None), P("grp", "seq", None), P("grp", "seq", None)),
        check_vma=False,
    )
```

```python
import math

import jax
import jax.numpy as jnp
from jax import lax
from jax.experimental import pallas as pl
from jax.experimental.pallas import tpu as pltpu
from jax.sharding import PartitionSpec as P

HEAD = 64
HEADS = 11
SEQ = 16
GRP = 48
ROWS = 128
PAIRS = 64
D = 1408
ATT = 704
PRED = 384
SHARD = 88
LO = 768
SLAB = 4
BURST = 4
SLOTS = GRP * SLAB

keep_rate = 0.9
epsilon = 1e-05

F32 = jnp.float32
BF16 = jnp.bfloat16


def normalize(values):
    center = values - jnp.mean(values, axis=-1, keepdims=True)
    variance = jnp.mean(center * center, axis=-1, keepdims=True)
    inverse = lax.rsqrt(variance + epsilon)
    return center * inverse, inverse


def dot(a, b):
    return jnp.dot(a, b, preferred_element_type=F32)


def dot_t(a, b):
    return lax.dot_general(a, b, (((1,), (1,)), ((), ())), preferred_element_type=F32)


def iota(shape, axis):
    return lax.broadcasted_iota(jnp.int32, shape, axis)


def slot_rows(own_row, mask_row):
    shape = (PAIRS, PAIRS)
    down, across = iota(shape, 0), iota(shape, 1)
    same = down == across

    def turned(row):
        return jnp.broadcast_to(
            jnp.sum(jnp.where(same, row, 0.0), axis=1, keepdims=True), shape
        )

    own_across = jnp.broadcast_to(own_row, shape)
    live_across = jnp.broadcast_to(mask_row, shape)
    own_down, live_down = turned(own_across), turned(live_across)
    equal = own_down == own_across
    rank_row = jnp.sum(
        jnp.where(equal & (down < across), live_down, 0.0), axis=0, keepdims=True
    )
    rank_col = jnp.sum(
        jnp.where(equal & (across < down), live_across, 0.0), axis=1, keepdims=True
    )
    slot_row = jnp.where(mask_row > 0.5, own_across[:1] * 2.0 + rank_row, -1.0)
    slot_col = jnp.where(live_down[:, :1] > 0.5, own_down[:, :1] * 2.0 + rank_col, -1.0)
    shape = (PAIRS, ROWS)
    token_row = jnp.sum(
        jnp.where(
            iota(shape, 0) == lax.shift_right_logical(iota(shape, 1), 1),
            jnp.broadcast_to(slot_col, shape),
            0.0,
        ),
        axis=0,
        keepdims=True,
    )
    shape = (ROWS, PAIRS)
    token_col = jnp.sum(
        jnp.where(
            lax.shift_right_logical(iota(shape, 0), 1) == iota(shape, 1),
            jnp.broadcast_to(slot_row, shape),
            0.0,
        ),
        axis=1,
        keepdims=True,
    )
    return token_row, token_col


def dispatch_tables(own_row, mask_row):
    token_row, token_col = slot_rows(own_row, mask_row)
    shape = (SLOTS, ROWS)
    spread = jnp.where(
        (
            lax.shift_right_logical(iota(shape, 0), 1)
            == jnp.broadcast_to(token_row, shape).astype(jnp.int32)
        )
        & (lax.bitwise_and(iota(shape, 0), 1) == lax.bitwise_and(iota(shape, 1), 1)),
        1.0,
        0.0,
    ).astype(BF16)
    shape = (ROWS, SLOTS)
    gather = jnp.where(
        (
            lax.shift_right_logical(iota(shape, 1), 1)
            == jnp.broadcast_to(token_col, shape).astype(jnp.int32)
        )
        & (lax.bitwise_and(iota(shape, 0), 1) == lax.bitwise_and(iota(shape, 1), 1)),
        1.0,
        0.0,
    ).astype(BF16)
    return spread, gather


def kernel(
    tok_hbm,
    tkv_hbm,
    ckv_hbm,
    qw_hbm,
    hid_hbm,
    pw_hbm,
    mask_hbm,
    own_hbm,
    nkv_ref,
    tgt_ref,
    pg_ref,
    tok_ref,
    tkv_ref,
    ckv_ref,
    qw_ref,
    hid_ref,
    pw_ref,
    mask_ref,
    own_ref,
    load_sem,
    wbuf,
    chunks,
    acc,
    queries,
    head_out,
    head_in,
    values_one,
    att_out,
    att_in,
    spread,
    gather,
    hid_out,
    hid_in,
    tgt_out,
    tgt_in,
    grad_out,
    grad_in,
    predicted,
    normed_h,
    inverses,
    w_send,
    w_recv,
    head_send,
    head_recv,
    att_send,
    att_recv,
    hid_send,
    hid_recv,
    tgt_send,
    tgt_recv,
    grad_send,
    grad_recv,
):
    loads = [
        pltpu.make_async_copy(src, dst, load_sem.at[i])
        for i, (src, dst) in enumerate(
            (
                (tkv_hbm, tkv_ref),
                (ckv_hbm, ckv_ref),
                (tok_hbm, tok_ref),
                (qw_hbm, qw_ref),
                (mask_hbm, mask_ref),
                (own_hbm, own_ref),
                (hid_hbm, hid_ref),
                (pw_hbm, pw_ref),
            )
        )
    ]
    for load in loads:
        load.start()
    me = lax.axis_index("seq")
    mine = lax.axis_index("grp")
    core = lax.rem(me, 2)
    x = lax.rem(me // 2, 4)
    y = me // 8
    z = mine // 4
    yh = lax.rem(mine, 4)

    def place(xx, yy, cc):
        return (lax.rem(xx, 4) + yy * 4) * 2 + cc

    right, left, far = place(x + 1, y, core), place(x + 3, y, core), place(x + 2, y, core)
    across = place(x, 1 - y, core)
    right_p, left_p, far_p = (
        place(x + 1, 1 - y, core),
        place(x + 3, 1 - y, core),
        place(x + 2, 1 - y, core),
    )
    twin = place(x, y, 1 - core)
    up_grp = z * 4 + lax.rem(yh + y, 4)
    down_grp = z * 4 + lax.rem(yh + 3 * (1 - y), 4)
    other_grp = z * 4 + lax.rem(yh + 3 + 2 * y, 4)

    def lane_of(to_yh):
        return jnp.where(lax.rem(to_yh - yh + 4, 4) == 2, across, me)

    barrier = pltpu.get_barrier_semaphore()

    @pl.loop(1, SEQ)
    def _(k):
        pl.semaphore_signal(barrier, inc=1, device_id={"seq": lax.rem(me + k, SEQ), "grp": mine})

    @pl.loop(1, GRP)
    def _(k):
        to = lax.rem(mine + k, GRP)
        pl.semaphore_signal(
            barrier, inc=1, device_id={"seq": lane_of(lax.rem(to, 4)), "grp": to}
        )

    pl.semaphore_signal(barrier, inc=1, device_id={"seq": across, "grp": other_grp})

    loads[0].wait()
    loads[1].wait()
    blended = (
        keep_rate * tkv_ref[...].astype(F32) + (1.0 - keep_rate) * ckv_ref[...].astype(F32)
    ).astype(BF16)
    nkv_ref[...] = blended
    wbuf[me] = blended
    pl.semaphore_wait(barrier, SEQ - 1 + GRP - 1 + 1)

    started = []

    def push(ref, slot, seq, grp):
        copy = pltpu.make_async_remote_copy(
            src_ref=ref,
            dst_ref=ref,
            send_sem=w_send.at[len(started)],
            recv_sem=w_recv.at[slot],
            device_id={"seq": seq, "grp": grp},
        )
        copy.start()
        started.append(copy)

    def arrive(ref, slot):
        pltpu.make_async_remote_copy(
            src_ref=ref,
            dst_ref=ref,
            send_sem=w_send.at[0],
            recv_sem=w_recv.at[slot],
            device_id={"seq": twin, "grp": mine},
        ).wait_recv()

    def lo(block):
        return wbuf.at[block, :, pl.ds(0, LO)]

    def hi(block):
        return wbuf.at[block, :, pl.ds(LO, D - LO)]

    push(lo(me), 0, right, mine)
    push(hi(me), 3, left, mine)
    push(lo(me), 4, across, up_grp)
    push(hi(me), 5, across, down_grp)
    push(hi(me), 1, right, mine)
    push(lo(me), 2, left, mine)
    push(wbuf.at[me], 14, twin, mine)

    loads[2].wait()
    normed = normalize(tok_ref[...].astype(F32))[0]
    for s in range(SEQ):
        chunks[s] = normed[:, s * SHARD : (s + 1) * SHARD].astype(BF16)
    normed_b = normed.astype(BF16)
    twin_of = 1 - 2 * core

    def term(block):
        return dot(chunks[block], wbuf[block])

    arrive(lo(left), 0)
    push(lo(left), 6, right, mine)
    push(lo(left), 8, across, up_grp)
    arrive(hi(right), 3)
    push(hi(right), 7, left, mine)
    push(hi(right), 11, across, down_grp)
    arrive(lo(across), 4)
    arrive(hi(across), 5)
    push(wbuf.at[across], 17, twin, mine)
    loads[3].wait()
    queries[...] = dot_t(normed_b, qw_ref[...])
    arrive(hi(left), 1)
    push(hi(left), 9, across, up_grp)
    push(wbuf.at[left], 15, twin, mine)
    arrive(lo(right), 2)
    push(lo(right), 10, across, down_grp)
    push(wbuf.at[right], 16, twin, mine)
    arrive(wbuf.at[twin], 14)
    acc[...] = term(me) + term(twin) + term(across)
    arrive(lo(left_p), 8)
    push(lo(left_p), 12, right, mine)
    arrive(hi(right_p), 11)
    push(hi(right_p), 13, left, mine)
    acc[...] += term(left) + term(right)
    arrive(lo(far), 6)
    arrive(hi(far), 7)
    push(wbuf.at[far], 18, twin, mine)
    arrive(wbuf.at[left + twin_of], 15)
    arrive(wbuf.at[right + twin_of], 16)
    arrive(wbuf.at[across + twin_of], 17)
    acc[...] += term(far) + term(left + twin_of) + term(right + twin_of) + term(across + twin_of)
    arrive(hi(left_p), 9)
    push(wbuf.at[left_p], 19, twin, mine)
    arrive(lo(right_p), 10)
    push(wbuf.at[right_p], 20, twin, mine)
    arrive(wbuf.at[far + twin_of], 18)
    acc[...] += term(left_p) + term(right_p) + term(far + twin_of)
    for load in loads[4:]:
        load.wait()
    spread[...], gather[...] = dispatch_tables(
        own_ref[...].astype(F32), mask_ref[...].astype(F32)
    )

    def to_slabs(rows):
        return rows.reshape(rows.shape[0] // SLAB, SLAB, rows.shape[1]).astype(BF16)

    hid_out[...] = to_slabs(dot(spread[...], hid_ref[...]))
    arrive(wbuf.at[left_p + twin_of], 19)
    arrive(wbuf.at[right_p + twin_of], 20)
    acc[...] += term(left_p + twin_of) + term(right_p + twin_of)
    arrive(lo(far_p), 12)
    push(lo(far_p), 21, twin, mine)
    arrive(hi(far_p), 13)
    push(hi(far_p), 22, twin, mine)
    acc[...] += term(far_p)
    arrive(lo(far_p + twin_of), 21)
    arrive(hi(far_p + twin_of), 22)
    acc[...] += term(far_p + twin_of)

    def head_place(h):
        return 2 * h if h < 8 else 1 + 4 * (h - 8)

    for h in range(HEADS):
        k_h = acc[:, h * HEAD : (h + 1) * HEAD]
        v_h = acc[:, ATT + h * HEAD : ATT + (h + 1) * HEAD]
        q_h = queries[:, h * HEAD : (h + 1) * HEAD]
        head_out[h, :ROWS] = jnp.concatenate([v_h, k_h], axis=1).astype(BF16)
        head_out[h, ROWS:] = jnp.concatenate([q_h[PAIRS:], q_h[:PAIRS]], axis=1).astype(BF16)
        to = head_place(h)

        @pl.when(me != to)
        def _():
            pltpu.make_async_remote_copy(
                src_ref=head_out.at[h],
                dst_ref=head_in.at[me],
                send_sem=head_send.at[h],
                recv_sem=head_recv.at[me],
                device_id={"seq": to, "grp": mine},
            ).start()

        @pl.when(me == to)
        def _():
            pltpu.make_async_copy(head_out.at[h], head_in.at[me], head_recv.at[me]).start()

    def outward(way):
        out, into, send, recv = way

        @pl.loop(0, GRP // 4 - 1)
        def _(m):
            dz = GRP // 8 + (m + 1) // 2 * (1 - 2 * lax.rem(m, 2))
            base = lax.rem(z + dz, GRP // 4) * 4
            slot = (GRP // 4 - dz) * 4 + yh
            for c in range(4):
                pltpu.make_async_remote_copy(
                    src_ref=out.at[base + c],
                    dst_ref=into.at[slot],
                    send_sem=send.at[m * 4 + c],
                    recv_sem=recv.at[slot],
                    device_id={"seq": lane_of(c), "grp": base + c},
                ).start()

    def outward_near(way):
        out, into, send, recv = way

        @pl.loop(1, 4)
        def _(k):
            to = z * 4 + lax.rem(yh + k, 4)
            pltpu.make_async_remote_copy(
                src_ref=out.at[to],
                dst_ref=into.at[yh],
                send_sem=send.at[GRP - 5 + k],
                recv_sem=recv.at[yh],
                device_id={"seq": jnp.where(k == 2, across, me), "grp": to},
            ).start()

        pltpu.make_async_copy(out.at[mine], into.at[yh], recv.at[yh]).start()

    def exchange(way):
        outward(way)
        outward_near(way)

    def received(way, first, last):
        out, into, send, recv = way

        @pl.loop(first, last)
        def _(k):
            pltpu.make_async_copy(out.at[k], into.at[k], recv.at[k]).wait()

    def sent(way, first, last):
        out, into, send, recv = way

        @pl.loop(first, last)
        def _(k):
            pltpu.make_async_copy(out.at[k], into.at[k], send.at[k]).wait()

    def homeward(first, last):
        @pl.loop(first // 4, last // 4)
        def _(dz):
            base = lax.rem(z + dz, GRP // 4) * 4
            for c in range(4):
                pltpu.make_async_remote_copy(
                    src_ref=grad_out.at[dz * 4 + c],
                    dst_ref=grad_in.at[mine],
                    send_sem=grad_send.at[dz * 4 + c],
                    recv_sem=grad_recv.at[mine],
                    device_id={"seq": lane_of(c), "grp": base + c},
                ).start()

    def homeward_near():
        @pl.loop(1, 4)
        def _(k):
            j = lax.rem(yh + k, 4)
            pltpu.make_async_remote_copy(
                src_ref=grad_out.at[j],
                dst_ref=grad_in.at[mine],
                send_sem=grad_send.at[j],
                recv_sem=grad_recv.at[mine],
                device_id={"seq": jnp.where(k == 2, across, me), "grp": z * 4 + j},
            ).start()

        pltpu.make_async_copy(grad_out.at[yh], grad_in.at[mine], grad_recv.at[mine]).start()

    hid_way = (hid_out, hid_in, hid_send, hid_recv)
    tgt_way = (tgt_out, tgt_in, tgt_send, tgt_recv)
    grad_way = (grad_out, grad_in, grad_send, grad_recv)

    exchange(hid_way)

    even = lax.rem(me, 2) == 0
    is_head = even | ((lax.rem(me, 4) == 1) & (me < 12))
    my_head = jnp.where(even, me // 2, 8 + me // 4)

    @pl.when(is_head)
    def _():
        lane = iota((ROWS, 2 * HEAD), 1)

        @pl.loop(0, SEQ)
        def _(t):
            pltpu.make_async_copy(head_out.at[0], head_in.at[t], head_recv.at[t]).wait()
            block = head_in[t, :ROWS].astype(F32)
            values_one[t] = jnp.where(lane < HEAD, block, 1.0).astype(BF16)

        rate = math.log2(math.e) / math.sqrt(HEAD)

        @pl.loop(0, SEQ // BURST)
        def _(i):
            zero = jnp.zeros((PAIRS, HEAD), BF16)
            parts = []
            for j in range(BURST):
                packed = head_in[BURST * i + j, ROWS:]
                parts.append(jnp.concatenate([zero, packed[:, HEAD:]], axis=1))
                parts.append(jnp.concatenate([zero, packed[:, :HEAD]], axis=1))
            q = jnp.concatenate(parts, axis=0)
            kv = head_in[:, :ROWS].reshape(SEQ * ROWS, 2 * HEAD)
            score = dot_t(q, kv)
            expo = jnp.exp2(score * rate).astype(BF16)
            added = dot(expo, values_one[...].reshape(SEQ * ROWS, 2 * HEAD))
            attended = added[:, :HEAD] / added[:, HEAD:]
            for j in range(BURST):
                rows = attended[j * ROWS : (j + 1) * ROWS]
                att_out[BURST * i + j] = jnp.concatenate(
                    [rows[:PAIRS], rows[PAIRS:]], axis=1
                ).astype(BF16)

            @pl.loop(0, BURST)
            def _(k):
                to = BURST * i + lax.rem(me + k, BURST)

                @pl.when(me != to)
                def _():
                    pltpu.make_async_remote_copy(
                        src_ref=att_out.at[to],
                        dst_ref=att_in.at[my_head],
                        send_sem=att_send.at[to],
                        recv_sem=att_recv.at[my_head],
                        device_id={"seq": to, "grp": mine},
                    ).start()

                @pl.when(me == to)
                def _():
                    pltpu.make_async_copy(
                        att_out.at[to], att_in.at[my_head], att_recv.at[my_head]
                    ).start()

    @pl.loop(0, HEADS)
    def _(h):
        pltpu.make_async_copy(att_out.at[0], att_in.at[h], att_recv.at[h]).wait()

    top = jnp.concatenate([att_in[h][:, :HEAD].astype(F32) for h in range(HEADS)], axis=1)
    low = jnp.concatenate([att_in[h][:, HEAD:].astype(F32) for h in range(HEADS)], axis=1)
    attended = jnp.concatenate([top, low], axis=0)
    targets = normalize(attended)[0]
    tgt_out[...] = to_slabs(dot(spread[...], targets.astype(BF16)))
    exchange(tgt_way)
    tgt_ref[...] = targets.T.astype(BF16)

    received(hid_way, 0, GRP)
    owned, inverse = normalize(hid_in[...].reshape(SLOTS, PRED).astype(F32))
    normed_h[...] = owned
    inverses[...] = inverse
    predicted[...] = dot_t(owned.astype(BF16), pw_ref[...])

    for first, last in ((16, 36), (0, 16), (36, 48)):
        rows = slice(first * SLAB, last * SLAB)
        received(tgt_way, first, last)
        landed = tgt_in[first:last].reshape((last - first) * SLAB, ATT).astype(F32)
        upstream = dot((predicted[rows] - landed).astype(BF16), pw_ref[...])
        own = normed_h[rows]
        upstream_mean = jnp.mean(upstream, axis=-1, keepdims=True)
        cross_mean = jnp.mean(upstream * own, axis=-1, keepdims=True)
        grad_out[first:last] = to_slabs(
            inverses[rows] * (upstream - upstream_mean - own * cross_mean)
        )
        if first == 0:
            homeward(4, last)
            homeward_near()
        else:
            homeward(first, last)

    received(grad_way, 0, GRP)
    pg_ref[...] = dot(gather[...], grad_in[...].reshape(SLOTS, PRED)).astype(BF16)

    for copy in started:
        copy.wait_send()
    for h in range(HEADS):

        @pl.when(me != head_place(h))
        def _():
            pltpu.make_async_copy(head_out.at[h], head_in.at[0], head_send.at[h]).wait()

    @pl.when(is_head)
    def _():
        @pl.loop(1, SEQ)
        def _(k):
            to = lax.rem(me + k, SEQ)
            pltpu.make_async_copy(att_out.at[to], att_in.at[0], att_send.at[to]).wait()

    sent(hid_way, 0, GRP - 1)
    sent(tgt_way, 0, GRP - 1)
    sent(grad_way, 4, GRP)

    @pl.loop(1, 4)
    def _(k):
        j = lax.rem(yh + k, 4)
        pltpu.make_async_copy(grad_out.at[j], grad_in.at[j], grad_send.at[j]).wait()


def finish(nkv_in, tgt_in, pg_in, nkv_out, tgt_out, pg_out, sem):
    copies = [
        pltpu.make_async_copy(src, dst, sem.at[i])
        for i, (src, dst) in enumerate(((tgt_in, tgt_out), (nkv_in, nkv_out), (pg_in, pg_out)))
    ]
    for copy in copies:
        copy.start()
    for copy in copies:
        copy.wait()


def shards(
    tokens, target_kv, context_kv, query_weight, pred_hidden, pred_weight, target_mask, owners
):
    vmem = pl.BlockSpec(memory_space=pltpu.VMEM)
    dma = pltpu.SemaphoreType.DMA
    results = pl.pallas_call(
        kernel,
        out_shape=(
            pltpu.VMEM((SHARD, D), BF16),
            pltpu.VMEM((ATT, ROWS), BF16),
            pltpu.VMEM((ROWS, PRED), BF16),
        ),
        in_specs=[pl.BlockSpec(memory_space=pl.ANY)] * 8,
        out_specs=(vmem,) * 3,
        scratch_shapes=[
            pltpu.VMEM((ROWS, D), BF16),
            pltpu.VMEM((SHARD, D), BF16),
            pltpu.VMEM((SHARD, D), BF16),
            pltpu.VMEM((ATT, D), BF16),
            pltpu.VMEM((ROWS, PRED), BF16),
            pltpu.VMEM((ATT, PRED), BF16),
            pltpu.VMEM((1, PAIRS), jnp.int32),
            pltpu.VMEM((1, PAIRS), jnp.int32),
            dma((8,)),
            pltpu.VMEM((SEQ, SHARD, D), BF16),
            pltpu.VMEM((SEQ, ROWS, SHARD), BF16),
            pltpu.VMEM((ROWS, D), F32),
            pltpu.VMEM((ROWS, ATT), F32),
            pltpu.VMEM((HEADS, ROWS + PAIRS, 2 * HEAD), BF16),
            pltpu.VMEM((SEQ, ROWS + PAIRS, 2 * HEAD), BF16),
            pltpu.VMEM((SEQ, ROWS, 2 * HEAD), BF16),
            pltpu.VMEM((SEQ, PAIRS, 2 * HEAD), BF16),
            pltpu.VMEM((HEADS, PAIRS, 2 * HEAD), BF16),
            pltpu.VMEM((SLOTS, ROWS), BF16),
            pltpu.VMEM((ROWS, SLOTS), BF16),
            pltpu.VMEM((GRP, SLAB, PRED), BF16),
            pltpu.VMEM((GRP, SLAB, PRED), BF16),
            pltpu.VMEM((GRP, SLAB, ATT), BF16),
            pltpu.VMEM((GRP, SLAB, ATT), BF16),
            pltpu.VMEM((GRP, SLAB, PRED), BF16),
            pltpu.VMEM((GRP, SLAB, PRED), BF16),
            pltpu.VMEM((SLOTS, ATT), F32),
            pltpu.VMEM((SLOTS, PRED), F32),
            pltpu.VMEM((SLOTS, 1), F32),
            dma((23,)),
            dma((23,)),
            dma((HEADS,)),
            dma((SEQ,)),
            dma((SEQ,)),
            dma((HEADS,)),
            dma((GRP,)),
            dma((GRP,)),
            dma((GRP,)),
            dma((GRP,)),
            dma((GRP,)),
            dma((GRP,)),
        ],
        compiler_params=pltpu.CompilerParams(
            collective_id=0, has_side_effects=True, vmem_limit_bytes=56 * 1024 * 1024
        ),
        cost_estimate=pl.CostEstimate(
            flops=2_000_000_000, bytes_accessed=5_000_000, transcendentals=3_000_000
        ),
        name="attend_and_route",
    )(
        *(
            pltpu.with_memory_space_constraint(argument, pltpu.HBM)
            for argument in (
                tokens[0],
                target_kv,
                context_kv,
                query_weight,
                pred_hidden[0],
                pred_weight[0],
                target_mask,
                owners[0].reshape(1, PAIRS),
            )
        )
    )
    anywhere = pl.BlockSpec(memory_space=pl.ANY)
    new_kv, targets, pred_grad = pl.pallas_call(
        finish,
        out_shape=tuple(jax.ShapeDtypeStruct(r.shape, r.dtype) for r in results),
        in_specs=[anywhere] * 3,
        out_specs=(anywhere,) * 3,
        scratch_shapes=[dma((3,))],
        name="finish",
    )(*(pltpu.with_memory_space_constraint(r, pltpu.VMEM) for r in results))
    return new_kv, targets.T[None], pred_grad[None]


def solution(mesh):
    placed = (
        P("grp", "seq", None),
        P("seq", None),
        P("seq", None),
        P(),
        P("grp", "seq", None),
        P("grp", None, None),
        P("grp", "seq"),
        P("grp", "seq", None),
    )
    return jax.shard_map(
        shards,
        mesh=mesh,
        in_specs=placed,
        out_specs=(P("seq", None), P("grp", "seq", None), P("grp", "seq", None)),
        check_vma=False,
    )
```
